768 devices in a mesh: pb: 96 (over x, z, core), pa: 8 (over y).
Axes of the slice: x: 4, y: 8, z: 12, core: 2. Of those that a mesh axis runs over, the one named last changes fastest.
Arguments:
- queries: bfloat16 [12288, 4096], P('pb'), may hold values from -0.09375 to 0.09375
- positives: bfloat16 [12288, 4096], P(('pb', 'pa')), may hold values from -0.09375 to 0.09375
- negative_pool: bfloat16 [768, 4096], P('pa'), may hold values from -0.09375 to 0.09375
- negatives: int32 [12288, 7], P('pb'), may hold values from 0 to 767
Outputs:
- query_grad: float32 [12288, 4096], P(('pb', 'pa'))
- positive_grad: float32 [12288, 4096], P(('pb', 'pa'))
- pool_grad: float32 [8, 96, 4096], P('pa', 'pb')
- losses: float32 [12288], P(('pb', 'pa'))
The draws below stay inside these ranges and needn't reach their ends.
All inputs are finite; a program needn't handle non-finite values.
Results may differ from the reference program's by a relative error of at most 0.0065.
Values sent between devices are 32-bit elements; how exact they have to be, the bound alone decides.
A program may use at most 32 MiB of HBM per device.

```python
import math
import jax
import jax.numpy as jnp
import numpy as np
from jax import lax

D = 4096
NEG = 7
Q_ROW = 128
PA_ROWS = 96
QUERIES = 12288
POOL = 768
BLOCKS = 8
N_PB = 96


def set_ends(array, rng, low, largest):
    place = [jax.random.randint(jax.random.fold_in(rng, axis), (), 0, length) for axis, length in enumerate(array.shape)]
    widest = array.shape.index(max(array.shape))
    beside = place[:widest] + [(place[widest] + 1) % array.shape[widest]] + place[widest + 1:]
    return array.at[tuple(place)].set(low).at[tuple(beside)].set(largest)


def levels(own_key, shape, cuts, smallest, high):
    def one(position, blocks):
        draws = jax.random.uniform(jax.random.fold_in(jax.random.fold_in(own_key, 6), position), (blocks,), jnp.float32, smallest / len(cuts), high / len(cuts))
        return jnp.repeat(jnp.exp(draws), shape[position] // blocks).reshape((-1,) + (1,) * (len(shape) - position - 1))

    loudness = one(*cuts[0])
    for cut in cuts[1:]:
        loudness = loudness * one(*cut)
    return loudness


def cumulative_ranks(number_of, skew):
    weights = [(1 << 20) // math.isqrt(grade ** skew) + 1 for grade in range(1, number_of + 1)]
    spread = 1 + sum(weights) // (1 << 30)
    return np.cumsum(np.array([max(1, weight // spread) for weight in weights]))


def skewed_ids(rng, extent, number_of, slope):
    grid = cumulative_ranks(number_of, slope)
    lot = jax.random.randint(jax.random.fold_in(rng, 1), extent, 0, int(grid[number_of - 1]))
    grade = jnp.searchsorted(jnp.asarray(grid, jnp.int32), lot, side="right")
    return jax.random.permutation(jax.random.fold_in(rng, 2), number_of)[grade].astype(jnp.int32)


def centred(rng, extent, deviation, limit, split=(), dtype=jnp.bfloat16):
    gain = levels(rng, extent, split, -0.22, 0.18) if split else 1.0
    values = jax.random.normal(rng, extent, jnp.float32) * deviation * gain
    return jnp.minimum(jnp.maximum(values, -limit), limit).astype(dtype)


def setup_inputs(seed: int = 0) -> dict:
    arg_keys = jax.random.split(jax.random.key(seed), 5)
    queries = centred(arg_keys[0], (QUERIES, D), D ** -0.5, 0.09375, ((0, 96),))
    positives = centred(arg_keys[1], (QUERIES, D), D ** -0.5, 0.09375, ((0, 768),))
    negative_pool = centred(arg_keys[2], (POOL, D), D ** -0.5, 0.09375, ((0, 8),))
    negatives = set_ends(skewed_ids(arg_keys[3], (QUERIES, NEG), POOL, 2), jax.random.fold_in(arg_keys[3], 3), 0, POOL - 1).astype(jnp.int32)
    return {"queries": queries, "positives": positives, "negative_pool": negative_pool, "negatives": negatives}


SOFTMAX_TEMPER = 0.02
EPSILON = 1e-06

def unit_rows(values):
    widened = values.astype(jnp.float32)
    scales = lax.rsqrt(lax.optimization_barrier(jnp.sum(widened * widened, axis=1)) + EPSILON)
    return (widened, scales, (widened * scales[:, None]).astype(jnp.bfloat16))

def norm_back(widened, scales, upstream):
    inner = lax.optimization_barrier(jnp.sum(widened * upstream, axis=1))
    cube = scales * scales * scales
    return scales[:, None] * upstream - (cube * inner)[:, None] * widened

def reference(queries, positives, negative_pool, negatives):
    query_wide, query_scale, normalized_queries = unit_rows(queries)
    passage_wide, passage_scale, normalized_passages = unit_rows(positives)
    bank_wide, bank_scale, normalized_bank_rows = unit_rows(negative_pool)
    grouped_queries = normalized_queries.reshape(N_PB, Q_ROW, D)
    grouped_passages = normalized_passages.reshape(N_PB, Q_ROW, D)
    grouped_ids = negatives.reshape(N_PB, Q_ROW, NEG)
    order_mask = lax.iota(jnp.int32, NEG)[None, :] < lax.iota(jnp.int32, NEG)[:, None]

    def group_step(bank_total, inputs):
        query_group_rows, passage_group_rows, group_ids = inputs
        batch_pair_scores = jnp.dot(query_group_rows, passage_group_rows.T, preferred_element_type=jnp.float32) / SOFTMAX_TEMPER
        selected_entries = normalized_bank_rows[group_ids]
        negative_bank_scores = jnp.einsum('oz,oiz->oi', query_group_rows.astype(jnp.float32), selected_entries.astype(jnp.float32)) / SOFTMAX_TEMPER
        inbatch_exp = jnp.exp(batch_pair_scores)
        bank_exp = jnp.exp(negative_bank_scores)
        partition_sums = lax.optimization_barrier(jnp.sum(inbatch_exp, axis=1)) + lax.optimization_barrier(jnp.sum(bank_exp, axis=1))
        multiplier = 1.0 / (SOFTMAX_TEMPER * partition_sums)
        same = group_ids[:, :, None] == group_ids[:, None, :]
        counts = lax.optimization_barrier(jnp.sum(same.astype(jnp.float32), axis=2))
        earlier = lax.optimization_barrier(jnp.sum((same & order_mask[None, :, :]).astype(jnp.int32), axis=2))
        batch_pair_weight = (inbatch_exp * multiplier[:, None]).astype(jnp.bfloat16)
        negative_bank_weight = jnp.where(earlier == 0, (bank_exp * counts * multiplier[:, None]).astype(jnp.bfloat16), jnp.zeros((), jnp.bfloat16))
        query_incoming_gradient = jnp.dot(batch_pair_weight, passage_group_rows, preferred_element_type=jnp.float32) + jnp.einsum('ys,ysn->yn', negative_bank_weight.astype(jnp.float32), selected_entries.astype(jnp.float32)) - passage_group_rows.astype(jnp.float32) / SOFTMAX_TEMPER
        passage_incoming_gradient = jnp.dot(batch_pair_weight.T, query_group_rows, preferred_element_type=jnp.float32) - query_group_rows.astype(jnp.float32) / SOFTMAX_TEMPER
        terms = negative_bank_weight.astype(jnp.float32)[:, :, None] * query_group_rows.astype(jnp.float32)[:, None, :]
        bank_total = bank_total + jax.ops.segment_sum(terms.reshape(Q_ROW * NEG, D), group_ids.reshape(Q_ROW * NEG), num_segments=POOL)
        losses = jnp.log(partition_sums) - jnp.diagonal(batch_pair_scores)
        return (bank_total, (query_incoming_gradient, passage_incoming_gradient, losses))
    bank_upstream, outputs = lax.scan(group_step, jnp.zeros((POOL, D), jnp.float32), (grouped_queries, grouped_passages, grouped_ids))
    query_up, passage_up, losses = outputs
    query_grad = norm_back(query_wide, query_scale, query_up.reshape(QUERIES, D))
    positive_grad = norm_back(passage_wide, passage_scale, passage_up.reshape(QUERIES, D))
    pool_grad = norm_back(bank_wide, bank_scale, bank_upstream).reshape(BLOCKS, PA_ROWS, D)
    return (query_grad, positive_grad, pool_grad, losses.reshape(QUERIES))
```

```python
import functools

import jax
import jax.numpy as jnp
from jax import lax
from jax.experimental import pallas as pl
from jax.experimental.pallas import tpu as pltpu
from jax.sharding import PartitionSpec as P

TEMPER = 0.02
INVERSE = 1.0 / TEMPER
EPSILON = 1e-06
NY, NX, NZ, NC = 8, 4, 12, 2
D = 4096
ROWS = 128
SHARE = 16
BANK = 96
NEG = 7
PIECE = 1024
NQ = D // PIECE
SUB = PIECE // 128
HALF_ROWS = BANK // NC
CHUNK = HALF_ROWS // NX
F32 = jnp.float32
BF16 = jnp.bfloat16
MESH = pl.DeviceIdType.MESH


def nt(left, right):
    return lax.dot_general(left, right, (((1,), (1,)), ((), ())), preferred_element_type=F32)


def iota(shape, dimension):
    return lax.broadcasted_iota(jnp.int32, shape, dimension)


def kernel(
    q_hbm, p_hbm, b_hbm, neg_hbm,
    qg_hbm, pg_hbm, bg_hbm, loss_hbm,
    rows, neg, part, own_row, passage_up, out_q, out_p, out_b, out_loss,
    totals, total_part, y_recv, bank, c_recv, x_recv1, x_recv2, z_send, z_recv,
    load_sem, store_sem, t_send_sem, t_recv_sem, y_send_sem, y_recv_sem,
    c_send_sem, c_recv_sem, x1_send_sem, x1_recv_sem, x2_send_sem, x2_recv_sem,
    z_send_sem, z_recv_sem,
):
    pb, pa = lax.axis_index("pb"), lax.axis_index("pa")
    core, z, x = pb % NC, (pb // NC) % NZ, pb // (NC * NZ)

    def at_y(step):
        return (pb, (pa + step) % NY)

    def at_x(step):
        return ((((x + step) % NX) * NZ + z) * NC + core, pa)

    def at_z(step):
        return ((x * NZ + (z + step) % NZ) * NC + core, pa)

    other_core = ((x * NZ + z) * NC + (1 - core), pa)

    barrier = pltpu.get_barrier_semaphore()
    partners = [other_core] + [at_x(1), at_x(NX - 1)]
    partners += [at_y(step) for step in range(1, NY)] + [at_z(step) for step in range(1, NZ)]
    for partner in partners:
        pl.semaphore_signal(barrier, inc=1, device_id=partner, device_id_type=MESH)

    loads = [
        pltpu.make_async_copy(q_hbm, rows.at[0:ROWS], load_sem.at[0]),
        pltpu.make_async_copy(b_hbm, rows.at[ROWS:ROWS + BANK], load_sem.at[1]),
        pltpu.make_async_copy(p_hbm, rows.at[ROWS + BANK:ROWS + BANK + SHARE], load_sem.at[2]),
        pltpu.make_async_copy(neg_hbm, neg, load_sem.at[3]),
    ]
    for load in loads:
        load.start()
    rows[ROWS + BANK + SHARE:2 * ROWS, :] = jnp.zeros((ROWS - BANK - SHARE, D), BF16)
    for load in loads:
        load.wait()

    lane = iota((ROWS, ROWS), 1)
    sub = iota((ROWS, ROWS), 0)
    eye = lane == sub

    def pick(mask, values, axis):
        return jnp.sum(jnp.where(mask, values, 0.0), axis=axis, keepdims=True)

    gram = nt(rows[...], rows[...])
    gram_q, raw, gram_c = gram[:ROWS, :ROWS], gram[:ROWS, ROWS:], gram[ROWS:, ROWS:]
    q_scale_col = lax.rsqrt(pick(eye, gram_q, 1) + EPSILON)
    q_scale_row = lax.rsqrt(pick(eye, gram_q, 0) + EPSILON)
    c_scale_row = lax.rsqrt(pick(eye, gram_c, 0) + EPSILON)
    scores = raw * (q_scale_col * INVERSE) * c_scale_row
    ids = jnp.where(lane < BANK, lane + pa * BANK, -1)
    counts = jnp.where((lane >= BANK) & (lane < BANK + SHARE), 1.0, 0.0)
    for k in range(NEG):
        counts = counts + jnp.where(neg[:, k:k + 1] == ids, 1.0, 0.0)
    exps = jnp.exp(scores) * counts
    exps_t = jnp.transpose(exps)
    total_part[...] = jnp.broadcast_to(jnp.sum(exps_t, axis=0, keepdims=True), (8, ROWS))
    totals[pl.ds(pa, 1)] = total_part[...][None]

    pl.semaphore_wait(barrier, len(partners))

    t_copies = []
    for step in range(1, NY):
        copy = pltpu.make_async_remote_copy(
            src_ref=total_part, dst_ref=totals.at[pa],
            send_sem=t_send_sem.at[step], recv_sem=t_recv_sem.at[pa],
            device_id=at_y(step), device_id_type=MESH)
        copy.start()
        t_copies.append(copy)

    weight = (exps * c_scale_row).astype(BF16)

    def part_piece(piece):
        for block in range(PIECE // 256):
            cols = pl.ds(piece * PIECE + block * 256, 256)
            part[:, cols] = jnp.dot(weight, rows[ROWS:, cols], preferred_element_type=F32)

    def y_rows(step):
        return pl.ds(pl.multiple_of(((pa + step) % NY) * SHARE, SHARE), SHARE)

    def y_distance(m):
        return 4 - (m + 1) // 2

    def y_pieces(s, m):
        half = s if m % 2 == 0 else 1 - s
        return (2 * half, 2 * half + 1)

    y_copies = []

    def y_copy(s, m, j):
        sign = 1 if s == 0 else -1
        piece = y_pieces(s, m)[j]
        return pltpu.make_async_remote_copy(
            src_ref=part.at[y_rows((sign * y_distance(m)) % NY), pl.ds(piece * PIECE, PIECE)],
            dst_ref=y_recv.at[s, m, j],
            send_sem=y_send_sem.at[s, m, j], recv_sem=y_recv_sem.at[s, m, j],
            device_id=at_y(sign % NY), device_id_type=MESH)

    def y_send(s, m, j):
        copy = y_copy(s, m, j)
        copy.start()
        y_copies.append(copy)

    part_piece(0)
    y_send(0, 0, 0)
    part_piece(2)
    y_send(1, 0, 0)
    part_piece(1)
    y_send(0, 0, 1)
    part_piece(3)
    y_send(1, 0, 1)
    for j in range(2):
        for s in range(2):
            y_send(s, 1, j)

    def y_step(m, j):
        for s in range(2):
            y_copy(s, m, j).wait_recv()
            sign = 1 if s == 0 else -1
            dest = y_rows((sign * (y_distance(m) - 1)) % NY)
            cols = pl.ds(y_pieces(s, m)[j] * PIECE, PIECE)
            part[dest, cols] = part[dest, cols] + y_recv[s, m, j]
            y_send(s, m + 2, j)

    for step in range(1, NY):
        origin = (pa + step) % NY
        pltpu.make_async_remote_copy(
            src_ref=total_part, dst_ref=totals.at[origin],
            send_sem=t_send_sem.at[step], recv_sem=t_recv_sem.at[origin],
            device_id=at_y(step), device_id_type=MESH).wait_recv()
    total_row = jnp.sum(totals[...], axis=0)[0:1, :]
    weight_t = (exps_t * (q_scale_row * INVERSE / total_row)).astype(BF16)
    order = jnp.where(sub < BANK, (sub % HALF_ROWS) * NC + sub // HALF_ROWS, sub)
    weight_t = jnp.dot(jnp.where(lane == order, 1.0, 0.0).astype(BF16), weight_t,
                       preferred_element_type=F32).astype(BF16)

    c_copies, x_copies, z_copies = [], [], []

    def core_rows(which):
        return pl.ds(pl.multiple_of(which * (HALF_ROWS * SUB), HALF_ROWS * SUB), HALF_ROWS * SUB)

    for piece in range(NQ):
        for block in range(PIECE // 256):
            cols = pl.ds(piece * PIECE + block * 256, 256)
            product = jnp.dot(weight_t, rows[0:ROWS, cols], preferred_element_type=F32)
            passage_up[:, cols] = product[BANK:BANK + SHARE, :]
            for r in range(BANK // 8):
                for c in range(2):
                    bank[piece, pl.ds(r * 8 * SUB + block * 2 + c, 8, stride=SUB), :] = (
                        product[r * 8:r * 8 + 8, c * 128:c * 128 + 128])
        copy = pltpu.make_async_remote_copy(
            src_ref=bank.at[piece, core_rows(1 - core)], dst_ref=c_recv.at[piece],
            send_sem=c_send_sem.at[piece], recv_sem=c_recv_sem.at[piece],
            device_id=other_core, device_id_type=MESH)
        copy.start()
        c_copies.append(copy)

    def x_rows(step):
        start = core * (HALF_ROWS * SUB) + ((x + step) % NX) * (CHUNK * SUB)
        return pl.ds(pl.multiple_of(start, CHUNK * SUB), CHUNK * SUB)

    def x_copy(stage, piece, s):
        sign = 1 if s == 0 else -1
        recv = x_recv1.at[piece] if stage == 1 else x_recv2.at[piece, s]
        send_sem = x1_send_sem.at[piece] if stage == 1 else x2_send_sem.at[piece, s]
        recv_sem = x1_recv_sem.at[piece] if stage == 1 else x2_recv_sem.at[piece, s]
        return pltpu.make_async_remote_copy(
            src_ref=bank.at[piece, x_rows(2 if stage == 1 else sign % NX)], dst_ref=recv,
            send_sem=send_sem, recv_sem=recv_sem,
            device_id=at_x(sign % NX), device_id_type=MESH)

    def x_send(stage, piece, s):
        copy = x_copy(stage, piece, s)
        copy.start()
        x_copies.append(copy)

    def c_step(batch):
        for s in range(2):
            piece = 2 * batch + s
            c_copies[piece].wait_recv()
            own = core_rows(core)
            bank[piece, own, :] = bank[piece, own, :] + c_recv[piece]
            x_send(1, piece, s)
        for s in range(2):
            x_send(2, 2 * batch + 1 - s, s)

    def x1_step(batch):
        for s in range(2):
            piece = 2 * batch + s
            sign = 1 if s == 0 else -1
            x_copy(1, piece, s).wait_recv()
            dest = x_rows(sign % NX)
            bank[piece, dest, :] = bank[piece, dest, :] + x_recv1[piece]
            x_send(2, piece, s)

    def z_copy(batch, step):
        return pltpu.make_async_remote_copy(
            src_ref=z_send.at[batch, (z + step) % NZ], dst_ref=z_recv.at[batch, z],
            send_sem=z_send_sem.at[batch, step], recv_sem=z_recv_sem.at[batch, z],
            device_id=at_z(step), device_id_type=MESH)

    def x2_step(batch):
        for s in range(2):
            piece = 2 * batch + s
            for t in range(2):
                x_copy(2, piece, t).wait_recv()
            total = bank[piece, x_rows(0), :] + x_recv2[piece, 0] + x_recv2[piece, 1]
            z_send[batch, :, s * SUB:(s + 1) * SUB, :] = total.reshape(CHUNK, SUB, 128)
        for step in range(1, NZ):
            copy = z_copy(batch, step)
            copy.start()
            z_copies.append(copy)
        z_recv[batch, pl.ds(z, 1)] = z_send[batch, pl.ds(z, 1)]

    def z_step(batch):
        for step in range(1, NZ):
            origin = (z + step) % NZ
            pltpu.make_async_remote_copy(
                src_ref=z_send.at[batch, 0], dst_ref=z_recv.at[batch, origin],
                send_sem=z_send_sem.at[batch, step], recv_sem=z_recv_sem.at[batch, origin],
                device_id=at_z(step), device_id_type=MESH).wait_recv()
        return jnp.sum(z_recv[batch], axis=0)

    def norm_back(wide, scale, upstream):
        inner = jnp.sum(wide * upstream, axis=1, keepdims=True)
        return scale * upstream - (scale * scale * scale * inner) * wide

    own_lane, own_sub = iota((SHARE, ROWS), 1), iota((SHARE, ROWS), 0)
    own_query = own_lane == own_sub + pa * SHARE
    q_scale_own = pick(own_query, q_scale_row, 1)
    total_own = pick(own_query, total_row, 1)
    p_scale_own = pick(own_lane == own_sub + BANK, c_scale_row, 1)

    y_step(0, 0)
    y_step(0, 1)
    c_step(0)
    y_step(1, 0)
    c_step(1)
    x1_step(0)
    y_step(1, 1)
    x1_step(1)
    x2_step(0)
    y_step(2, 0)
    x2_step(1)

    own_q_rows = pl.ds(pl.multiple_of(pa * SHARE, SHARE), SHARE)
    own_q = rows[own_q_rows, :].astype(F32)
    own_p = rows[ROWS + BANK:ROWS + BANK + SHARE, :].astype(F32)
    passage_v = passage_up[...] - own_q * (q_scale_own * INVERSE)
    out_p[...] = norm_back(own_p, p_scale_own, passage_v)
    store_p = pltpu.make_async_copy(out_p, pg_hbm, store_sem.at[0])
    store_p.start()
    own_score = pick(lane == sub - pa * SHARE + BANK, scores, 1)
    score_row = pick(lane == sub - pa * SHARE, own_score, 0)
    total_head = pick(own_lane == own_sub, total_own, 0)
    loss = jnp.log(jnp.where(own_lane[0:1] < SHARE, total_head, 1.0)) - score_row
    out_loss[...] = jnp.broadcast_to(loss, (8, ROWS))
    store_loss = pltpu.make_async_copy(out_loss, loss_hbm, store_sem.at[1])
    store_loss.start()

    y_step(2, 1)

    one_hot = jnp.where(iota((SHARE, ROWS), 1) == pb, 1.0, 0.0).astype(BF16)
    for block in range(D // 256):
        row = jnp.dot(one_hot, rows[ROWS:, block * 256:block * 256 + 256], preferred_element_type=F32)
        for c in range(2):
            own_row[block * 2 + c:block * 2 + c + 1, :] = row[0:1, c * 128:c * 128 + 128]

    y_step(3, 0)
    y_step(3, 1)
    y_step(4, 0)
    y_step(4, 1)

    wide = own_row[...]
    bank_v = jnp.concatenate([z_step(0), z_step(1)], axis=0)

    def whole(values):
        return jnp.sum(jnp.sum(values, axis=0, keepdims=True), axis=1, keepdims=True)

    scale = lax.rsqrt(whole(wide * wide) + EPSILON)
    out_b[...] = scale * bank_v - (scale * scale * scale * whole(wide * bank_v)) * wide
    store_b = pltpu.make_async_copy(out_b, bg_hbm, store_sem.at[2])
    store_b.start()

    inverse_own = INVERSE / total_own
    own = y_rows(0)
    inner = jnp.zeros((SHARE, 1), F32)
    for m in (5, 6):
        for j in range(2):
            for s in range(2):
                y_copy(s, m, j).wait_recv()
    for piece in range(NQ):
        half, j = piece // 2, piece % 2
        cols = pl.ds(piece * PIECE, PIECE)
        arrived = y_recv[0, 6 if half == 0 else 5, j] + y_recv[1, 5 if half == 0 else 6, j]
        value = (part[own, cols] + arrived) * inverse_own
        value = value - own_p[:, piece * PIECE:(piece + 1) * PIECE] * (p_scale_own * INVERSE)
        out_q[:, cols] = value
        inner = inner + jnp.sum(value * own_q[:, piece * PIECE:(piece + 1) * PIECE], axis=1, keepdims=True)
    out_q[...] = q_scale_own * out_q[...] - (q_scale_own * q_scale_own * q_scale_own * inner) * own_q
    store_q = pltpu.make_async_copy(out_q, qg_hbm, store_sem.at[3])
    store_q.start()

    for copy in t_copies + y_copies + c_copies + x_copies + z_copies:
        copy.wait_send()
    for store in (store_p, store_loss, store_b, store_q):
        store.wait()


def on_device(queries, positives, negative_pool, negatives):
    anywhere = pl.BlockSpec(memory_space=pl.ANY)
    dma = pltpu.SemaphoreType.DMA
    query_grad, positive_grad, pool_grad, losses = pl.pallas_call(
        kernel,
        out_shape=(
            jax.ShapeDtypeStruct((SHARE, D), F32),
            jax.ShapeDtypeStruct((SHARE, D), F32),
            jax.ShapeDtypeStruct((D // 128, 128), F32),
            jax.ShapeDtypeStruct((8, ROWS), F32),
        ),
        in_specs=[anywhere] * 4,
        out_specs=(anywhere,) * 4,
        scratch_shapes=[
            pltpu.VMEM((2 * ROWS, D), BF16),
            pltpu.VMEM((ROWS, NEG), jnp.int32),
            pltpu.VMEM((ROWS, D), F32),
            pltpu.VMEM((D // 128, 128), F32),
            pltpu.VMEM((SHARE, D), F32),
            pltpu.VMEM((SHARE, D), F32),
            pltpu.VMEM((SHARE, D), F32),
            pltpu.VMEM((D // 128, 128), F32),
            pltpu.VMEM((8, ROWS), F32),
            pltpu.VMEM((NY, 8, ROWS), F32),
            pltpu.VMEM((8, ROWS), F32),
            pltpu.VMEM((2, 7, 2, SHARE, PIECE), F32),
            pltpu.VMEM((NQ, BANK * SUB, 128), F32),
            pltpu.VMEM((NQ, HALF_ROWS * SUB, 128), F32),
            pltpu.VMEM((NQ, CHUNK * SUB, 128), F32),
            pltpu.VMEM((NQ, 2, CHUNK * SUB, 128), F32),
            pltpu.VMEM((2, CHUNK, 2 * SUB, 128), F32),
            pltpu.VMEM((2, CHUNK, 2 * SUB, 128), F32),
            dma((4,)), dma((4,)), dma((NY,)), dma((NY,)),
            dma((2, 7, 2)), dma((2, 7, 2)),
            dma((NQ,)), dma((NQ,)), dma((NQ,)), dma((NQ,)),
            dma((NQ, 2)), dma((NQ, 2)), dma((2, NZ)), dma((2, NZ)),
        ],
        compiler_params=pltpu.CompilerParams(
            collective_id=0, has_side_effects=True, vmem_limit_bytes=40 * 1024 * 1024),
    )(queries, positives, negative_pool, negatives)
    return query_grad, positive_grad, pool_grad.reshape(1, 1, D), losses[0, :SHARE]


def solution(mesh):
    placed = (P("pb", None), P(("pb", "pa"), None), P("pa", None), P("pb", None))
    return jax.shard_map(
        on_device,
        mesh=mesh,
        in_specs=placed,
        out_specs=(
            P(("pb", "pa"), None),
            P(("pb", "pa"), None),
            P("pa", "pb", None),
            P(("pb", "pa")),
        ),
        check_vma=False,
    )
```

```python
import functools

import jax
import jax.numpy as jnp
from jax import lax
from jax.experimental import pallas as pl
from jax.experimental.pallas import tpu as pltpu
from jax.sharding import PartitionSpec as P

TEMPER = 0.02
INVERSE = 1.0 / TEMPER
EPSILON = 1e-06
NY, NX, NZ, NC = 8, 4, 12, 2
D = 4096
ROWS = 128
SHARE = 16
BANK = 96
NEG = 7
PIECE = 1024
THIN = 512
NT = D // THIN
NB = NT // 2
SUB = THIN // 128
HALF_ROWS = BANK // NC
CHUNK = HALF_ROWS // NX
F32 = jnp.float32
BF16 = jnp.bfloat16
MESH = pl.DeviceIdType.MESH


def nt(left, right):
    return lax.dot_general(left, right, (((1,), (1,)), ((), ())), preferred_element_type=F32)


def iota(shape, dimension):
    return lax.broadcasted_iota(jnp.int32, shape, dimension)


def kernel(
    q_hbm, p_hbm, b_hbm, neg_hbm,
    qg_hbm, pg_hbm, bg_hbm, loss_hbm,
    rows, neg, part, own_row, passage_up, out_q, out_p, out_b, out_loss,
    totals, total_part, y_recv, bank, c_recv, x_recv1, x_recv2, z_send, z_recv,
    load_sem, store_sem, t_send_sem, t_recv_sem, y_send_sem, y_recv_sem,
    c_send_sem, c_recv_sem, x1_send_sem, x1_recv_sem, x2_send_sem, x2_recv_sem,
    z_send_sem, z_recv_sem,
):
    pb, pa = lax.axis_index("pb"), lax.axis_index("pa")
    core, z, x = pb % NC, (pb // NC) % NZ, pb // (NC * NZ)

    def at_y(step):
        return (pb, (pa + step) % NY)

    def at_x(step):
        return ((((x + step) % NX) * NZ + z) * NC + core, pa)

    def at_z(step):
        return ((x * NZ + (z + step) % NZ) * NC + core, pa)

    other_core = ((x * NZ + z) * NC + (1 - core), pa)

    loads = []
    for half in range(2):
        cols = slice(half * (D // 2), (half + 1) * (D // 2))
        for i, (source, first, count) in enumerate(
                ((q_hbm, 0, ROWS), (b_hbm, ROWS, BANK), (p_hbm, ROWS + BANK, SHARE))):
            loads.append(pltpu.make_async_copy(
                source.at[:, cols], rows.at[first:first + count, cols], load_sem.at[half, i]))
    load_neg = pltpu.make_async_copy(neg_hbm, neg, load_sem.at[0, 3])
    for load in loads:
        load.start()
    load_neg.start()

    barrier = pltpu.get_barrier_semaphore()
    partners = [other_core] + [at_x(1), at_x(NX - 1)]
    partners += [at_y(step) for step in range(1, NY)] + [at_z(step) for step in range(1, NZ)]
    for partner in partners:
        pl.semaphore_signal(barrier, inc=1, device_id=partner, device_id_type=MESH)
    rows[ROWS + BANK + SHARE:2 * ROWS, :] = jnp.zeros((ROWS - BANK - SHARE, D), BF16)

    lane = iota((ROWS, ROWS), 1)
    sub = iota((ROWS, ROWS), 0)
    eye = lane == sub

    def pick(mask, values, axis):
        return jnp.sum(jnp.where(mask, values, 0.0), axis=axis, keepdims=True)

    gram_left, gram_c = 0.0, 0.0
    for half in range(2):
        for load in loads[3 * half:3 * half + 3]:
            load.wait()
        cols = slice(half * (D // 2), (half + 1) * (D // 2))
        gram_left = gram_left + nt(rows[:, cols], rows[:ROWS, cols])
        gram_c = gram_c + nt(rows[ROWS:, cols], rows[ROWS:, cols])
    gram_q, raw = gram_left[:ROWS], gram_left[ROWS:]
    load_neg.wait()
    q_scale_row = lax.rsqrt(pick(eye, gram_q, 0) + EPSILON)
    c_scale_col = lax.rsqrt(pick(eye, gram_c, 1) + EPSILON)
    c_scale_row = lax.rsqrt(pick(eye, gram_c, 0) + EPSILON)
    scores = raw * c_scale_col * (q_scale_row * INVERSE)
    ids = jnp.where(sub < BANK, sub + pa * BANK, -1)
    counts = jnp.where((sub >= BANK) & (sub < BANK + SHARE), 1.0, 0.0)
    for k in range(NEG):
        counts = counts + jnp.where(neg[k:k + 1, :] == ids, 1.0, 0.0)
    exps_t = jnp.exp(scores) * counts
    total_part[...] = jnp.broadcast_to(jnp.sum(exps_t, axis=0, keepdims=True), (8, ROWS))
    totals[pl.ds(pa, 1)] = total_part[...][None]

    pl.semaphore_wait(barrier, len(partners))

    for step in range(1, NY):
        copy = pltpu.make_async_remote_copy(
            src_ref=total_part, dst_ref=totals.at[pa],
            send_sem=t_send_sem, recv_sem=t_recv_sem,
            device_id=at_y(step), device_id_type=MESH)
        copy.start()

    weight = jnp.transpose(exps_t * c_scale_col).astype(BF16)

    def part_piece(piece):
        for block in range(PIECE // 256):
            cols = pl.ds(piece * PIECE + block * 256, 256)
            part[:, cols] = jnp.dot(weight, rows[ROWS:, cols], preferred_element_type=F32)

    def y_rows(step):
        return pl.ds(pl.multiple_of(((pa + step) % NY) * SHARE, SHARE), SHARE)

    def y_distance(m):
        return 4 - (m + 1) // 2

    def y_pieces(s, m):
        half = s if m % 2 == 0 else 1 - s
        return (2 * half, 2 * half + 1)

    y_copies = []

    def y_copy(s, m, j):
        sign = 1 if s == 0 else -1
        piece = y_pieces(s, m)[j]
        return pltpu.make_async_remote_copy(
            src_ref=part.at[y_rows((sign * y_distance(m)) % NY), pl.ds(piece * PIECE, PIECE)],
            dst_ref=y_recv.at[s, m, j],
            send_sem=y_send_sem.at[s, m, j], recv_sem=y_recv_sem.at[s, m, j],
            device_id=at_y(sign % NY), device_id_type=MESH)

    def y_send(s, m, j):
        copy = y_copy(s, m, j)
        copy.start()
        y_copies.append(copy)

    part_piece(0)
    y_send(0, 0, 0)
    part_piece(2)
    y_send(1, 0, 0)
    part_piece(1)
    y_send(0, 0, 1)
    part_piece(3)
    y_send(1, 0, 1)
    for j in range(2):
        for s in range(2):
            y_send(s, 1, j)

    def y_step(m, j):
        for s in range(2):
            y_copy(s, m, j).wait_recv()
            sign = 1 if s == 0 else -1
            dest = y_rows((sign * (y_distance(m) - 1)) % NY)
            cols = pl.ds(y_pieces(s, m)[j] * PIECE, PIECE)
            part[dest, cols] = part[dest, cols] + y_recv[s, m, j]
            y_send(s, m + 2, j)

    pltpu.make_async_copy(totals.at[1:NY], totals.at[1:NY], t_recv_sem).wait()
    total_row = jnp.sum(totals[...], axis=0)[0:1, :]
    weight_t = (exps_t * (q_scale_row * INVERSE / total_row)).astype(BF16)
    order = jnp.where(sub < BANK, (sub % HALF_ROWS) * NC + sub // HALF_ROWS, sub)
    weight_t = jnp.dot(jnp.where(lane == order, 1.0, 0.0).astype(BF16), weight_t,
                       preferred_element_type=F32).astype(BF16)

    c_copies, x_copies = [], []

    def core_rows(which):
        return pl.ds(pl.multiple_of(which * (HALF_ROWS * SUB), HALF_ROWS * SUB), HALF_ROWS * SUB)

    for piece in range(NT):
        for block in range(THIN // 256):
            cols = pl.ds(piece * THIN + block * 256, 256)
            product = jnp.dot(weight_t, rows[0:ROWS, cols], preferred_element_type=F32)
            passage_up[:, cols] = product[BANK:BANK + SHARE, :]
            for r in range(BANK // 8):
                for c in range(2):
                    bank[piece, pl.ds(r * 8 * SUB + block * 2 + c, 8, stride=SUB), :] = (
                        product[r * 8:r * 8 + 8, c * 128:c * 128 + 128])
        copy = pltpu.make_async_remote_copy(
            src_ref=bank.at[piece, core_rows(1 - core)], dst_ref=c_recv.at[piece],
            send_sem=c_send_sem.at[piece], recv_sem=c_recv_sem.at[piece],
            device_id=other_core, device_id_type=MESH)
        copy.start()
        c_copies.append(copy)

    def x_rows(step):
        start = core * (HALF_ROWS * SUB) + ((x + step) % NX) * (CHUNK * SUB)
        return pl.ds(pl.multiple_of(start, CHUNK * SUB), CHUNK * SUB)

    def x_copy(stage, piece, s):
        sign = 1 if s == 0 else -1
        recv = x_recv1.at[piece] if stage == 1 else x_recv2.at[piece, s]
        send_sem = x1_send_sem.at[piece] if stage == 1 else x2_send_sem.at[piece, s]
        recv_sem = x1_recv_sem.at[piece] if stage == 1 else x2_recv_sem.at[piece, s]
        return pltpu.make_async_remote_copy(
            src_ref=bank.at[piece, x_rows(2 if stage == 1 else sign % NX)], dst_ref=recv,
            send_sem=send_sem, recv_sem=recv_sem,
            device_id=at_x(sign % NX), device_id_type=MESH)

    def x_send(stage, piece, s):
        copy = x_copy(stage, piece, s)
        copy.start()
        x_copies.append(copy)

    def c_step(batch):
        for piece in (2 * batch, 2 * batch + 1):
            c_copies[piece].wait_recv()
            own = core_rows(core)
            bank[piece, own, :] = bank[piece, own, :] + c_recv[piece]

    def x_first(batch):
        for s in range(2):
            x_send(1, 2 * batch + s, s)
        for s in range(2):
            x_send(2, 2 * batch + 1 - s, s)

    def x1_step(batch):
        for s in range(2):
            piece = 2 * batch + s
            sign = 1 if s == 0 else -1
            x_copy(1, piece, s).wait_recv()
            dest = x_rows(sign % NX)
            bank[piece, dest, :] = bank[piece, dest, :] + x_recv1[piece]
            x_send(2, piece, s)

    def x2_step(batch):
        for s in range(2):
            piece = 2 * batch + s
            for t in range(2):
                x_copy(2, piece, t).wait_recv()
            total = bank[piece, x_rows(0), :] + x_recv2[piece, 0] + x_recv2[piece, 1]
            z_send[batch, :, s * SUB:(s + 1) * SUB, :] = total.reshape(CHUNK, SUB, 128)
        for step in range(1, NZ):
            pltpu.make_async_remote_copy(
                src_ref=z_send.at[batch, (z + step) % NZ], dst_ref=z_recv.at[batch, z],
                send_sem=z_send_sem.at[batch], recv_sem=z_recv_sem.at[batch],
                device_id=at_z(step), device_id_type=MESH).start()
        z_recv[batch, pl.ds(z, 1)] = z_send[batch, pl.ds(z, 1)]

    def z_step(batch):
        rest = z_recv.at[batch, 1:NZ]
        pltpu.make_async_copy(rest, rest, z_recv_sem.at[batch]).wait()
        return jnp.sum(z_recv[batch], axis=0)

    def norm_back(wide, scale, upstream):
        inner = jnp.sum(wide * upstream, axis=1, keepdims=True)
        return scale * upstream - (scale * scale * scale * inner) * wide

    own_lane, own_sub = iota((SHARE, ROWS), 1), iota((SHARE, ROWS), 0)
    own_query = own_lane == own_sub + pa * SHARE
    q_scale_own = pick(own_query, q_scale_row, 1)
    total_own = pick(own_query, total_row, 1)
    p_scale_own = pick(own_lane == own_sub + BANK, c_scale_row, 1)

    c_step(0)
    x_first(0)
    c_step(1)
    x_first(1)
    y_step(0, 0)
    c_step(2)
    c_step(3)
    x1_step(0)
    x_first(2)
    y_step(0, 1)
    x1_step(1)
    x_first(3)
    x2_step(0)
    y_step(1, 0)
    x1_step(2)
    x2_step(1)
    y_step(1, 1)
    x1_step(3)
    x2_step(2)
    y_step(2, 0)
    x2_step(3)

    own_q_rows = pl.ds(pl.multiple_of(pa * SHARE, SHARE), SHARE)
    own_q = rows[own_q_rows, :].astype(F32)
    own_p = rows[ROWS + BANK:ROWS + BANK + SHARE, :].astype(F32)
    passage_v = passage_up[...] - own_q * (q_scale_own * INVERSE)
    out_p[...] = norm_back(own_p, p_scale_own, passage_v)
    store_p = pltpu.make_async_copy(out_p, pg_hbm, store_sem.at[0])
    store_p.start()
    own_score = pick(own_query, scores[BANK:BANK + SHARE, :], 1)
    loss = pick(own_lane == own_sub, jnp.log(total_own) - own_score, 0)
    out_loss[...] = loss[:, :SHARE]
    store_loss = pltpu.make_async_copy(out_loss, loss_hbm, store_sem.at[1])
    store_loss.start()

    y_step(2, 1)

    one_hot = jnp.where(iota((SHARE, ROWS), 1) == pb, 1.0, 0.0).astype(BF16)
    for block in range(D // 256):
        row = jnp.dot(one_hot, rows[ROWS:, block * 256:block * 256 + 256], preferred_element_type=F32)
        for c in range(2):
            own_row[block * 2 + c:block * 2 + c + 1, :] = row[0:1, c * 128:c * 128 + 128]

    y_step(3, 0)
    y_step(3, 1)
    y_step(4, 0)
    y_step(4, 1)

    inverse_own = INVERSE / total_own
    own = y_rows(0)
    inner = jnp.zeros((SHARE, 1), F32)
    for m in (5, 6):
        for j in range(2):
            for s in range(2):
                y_copy(s, m, j).wait_recv()
    for piece in range(D // PIECE):
        half, j = piece // 2, piece % 2
        cols = pl.ds(piece * PIECE, PIECE)
        arrived = y_recv[0, 6 if half == 0 else 5, j] + y_recv[1, 5 if half == 0 else 6, j]
        value = (part[own, cols] + arrived) * inverse_own
        value = value - own_p[:, piece * PIECE:(piece + 1) * PIECE] * (p_scale_own * INVERSE)
        out_q[:, cols] = value
        inner = inner + jnp.sum(value * own_q[:, piece * PIECE:(piece + 1) * PIECE], axis=1, keepdims=True)
    out_q[...] = q_scale_own * out_q[...] - (q_scale_own * q_scale_own * q_scale_own * inner) * own_q
    store_q = pltpu.make_async_copy(out_q, qg_hbm, store_sem.at[3])
    store_q.start()

    def whole(values):
        return jnp.sum(jnp.sum(values, axis=0, keepdims=True), axis=1, keepdims=True)

    wide = own_row[...]
    scale = lax.rsqrt(whole(wide * wide) + EPSILON)
    for copy in y_copies + c_copies + x_copies:
        copy.wait_send()
    pltpu.make_async_copy(totals.at[1:NY], totals.at[1:NY], t_send_sem).wait()
    for batch in range(NB):
        rest = z_send.at[batch, 1:NZ]
        pltpu.make_async_copy(rest, rest, z_send_sem.at[batch]).wait()
    for store in (store_p, store_loss, store_q):
        store.wait()

    bank_v = jnp.concatenate([z_step(batch) for batch in range(NB)], axis=0)
    out_b[...] = scale * bank_v - (scale * scale * scale * whole(wide * bank_v)) * wide
    store_b = pltpu.make_async_copy(out_b, bg_hbm, store_sem.at[2])
    store_b.start()
    store_b.wait()


def hand_over(*refs):
    copies = [pltpu.make_async_copy(refs[i], refs[4 + i], refs[8].at[i]) for i in range(4)]
    for copy in copies:
        copy.start()
    for copy in copies:
        copy.wait()


def on_device(queries, positives, negative_pool, negatives):
    anywhere = pl.BlockSpec(memory_space=pl.ANY)
    dma = pltpu.SemaphoreType.DMA
    query_grad, positive_grad, pool_grad, losses = pl.pallas_call(
        kernel,
        out_shape=(
            jax.ShapeDtypeStruct((SHARE, D), F32),
            jax.ShapeDtypeStruct((SHARE, D), F32),
            jax.ShapeDtypeStruct((D // 128, 128), F32),
            jax.ShapeDtypeStruct((1, SHARE), F32),
        ),
        in_specs=[anywhere] * 4,
        out_specs=(anywhere,) * 4,
        scratch_shapes=[
            pltpu.VMEM((2 * ROWS, D), BF16),
            pltpu.VMEM((NEG, ROWS), jnp.int32),
            pltpu.VMEM((ROWS, D), F32),
            pltpu.VMEM((D // 128, 128), F32),
            pltpu.VMEM((SHARE, D), F32),
            pltpu.VMEM((SHARE, D), F32),
            pltpu.VMEM((SHARE, D), F32),
            pltpu.VMEM((D // 128, 128), F32),
            pltpu.VMEM((1, SHARE), F32),
            pltpu.VMEM((NY, 8, ROWS), F32),
            pltpu.VMEM((8, ROWS), F32),
            pltpu.VMEM((2, 7, 2, SHARE, PIECE), F32),
            pltpu.VMEM((NT, BANK * SUB, 128), F32),
            pltpu.VMEM((NT, HALF_ROWS * SUB, 128), F32),
            pltpu.VMEM((NT, CHUNK * SUB, 128), F32),
            pltpu.VMEM((NT, 2, CHUNK * SUB, 128), F32),
            pltpu.VMEM((NB, CHUNK, 2 * SUB, 128), F32),
            pltpu.VMEM((NB, CHUNK, 2 * SUB, 128), F32),
            dma((2, 4)), dma((4,)), dma, dma,
            dma((2, 7, 2)), dma((2, 7, 2)),
            dma((NT,)), dma((NT,)), dma((NT,)), dma((NT,)),
            dma((NT, 2)), dma((NT, 2)), dma((NB,)), dma((NB,)),
        ],
        compiler_params=pltpu.CompilerParams(
            collective_id=0, has_side_effects=True, vmem_limit_bytes=40 * 1024 * 1024),
    )(*[pltpu.with_memory_space_constraint(t, pltpu.HBM) for t in (queries, positives, negative_pool, negatives.T)])
    query_grad, positive_grad, pool_grad, losses = pl.pallas_call(
        hand_over,
        out_shape=(
            jax.ShapeDtypeStruct((SHARE, D), F32),
            jax.ShapeDtypeStruct((SHARE, D), F32),
            jax.ShapeDtypeStruct((D // 128, 128), F32),
            jax.ShapeDtypeStruct((1, SHARE), F32),
        ),
        in_specs=[anywhere] * 4,
        out_specs=(anywhere,) * 4,
        scratch_shapes=[dma((4,))],
        compiler_params=pltpu.CompilerParams(vmem_limit_bytes=4 * 1024 * 1024),
    )(query_grad, positive_grad, pool_grad, losses)
    return query_grad, positive_grad, pool_grad.reshape(1, 1, D), losses.reshape(SHARE)


def solution(mesh):
    placed = (P("pb", None), P(("pb", "pa"), None), P("pa", None), P("pb", None))
    return jax.shard_map(
        on_device,
        mesh=mesh,
        in_specs=placed,
        out_specs=(
            P(("pb", "pa"), None),
            P(("pb", "pa"), None),
            P("pa", "pb", None),
            P(("pb", "pa")),
        ),
        check_vma=False,
    )
```

```python
import functools

import jax
import jax.numpy as jnp
from jax import lax
from jax.experimental import pallas as pl
from jax.experimental.pallas import tpu as pltpu
from jax.sharding import PartitionSpec as P

TEMPER = 0.02
INVERSE = 1.0 / TEMPER
EPSILON = 1e-06
NY, NX, NZ, NC = 8, 4, 12, 2
D = 4096
ROWS = 128
SHARE = 16
BANK = 96
NEG = 7
PIECE = 1024
THIN = 512
NT = D // THIN
HUB = 9
NB = NT // 2
SUB = THIN // 128
HALF_ROWS = BANK // NC
CHUNK = HALF_ROWS // NX
F32 = jnp.float32
BF16 = jnp.bfloat16
MESH = pl.DeviceIdType.MESH


def nt(left, right):
    return lax.dot_general(left, right, (((1,), (1,)), ((), ())), preferred_element_type=F32)


def iota(shape, dimension):
    return lax.broadcasted_iota(jnp.int32, shape, dimension)


def kernel(
    q_hbm, p_hbm, b_hbm, neg_hbm,
    qg_hbm, pg_hbm, bg_hbm, loss_hbm,
    rows, neg, part, own_row, passage_up, out_q, out_p, out_b, out_loss,
    totals, total_part, y_recv, bank, c_recv, x_recv1, x_recv2, z_send, z_recv,
    load_sem, store_sem, t_send_sem, t_recv_sem, y_send_sem, y_recv_sem,
    c_send_sem, c_recv_sem, x1_send_sem, x1_recv_sem, x2_send_sem, x2_recv_sem,
    z_send_sem, z_recv_sem, all_here,
):
    pb, pa = lax.axis_index("pb"), lax.axis_index("pa")
    core, z, x = pb % NC, (pb // NC) % NZ, pb // (NC * NZ)

    def at_y(step):
        return (pb, (pa + step) % NY)

    def at_x(step):
        return ((((x + step) % NX) * NZ + z) * NC + core, pa)

    def at_z(step):
        return ((x * NZ + (z + step) % NZ) * NC + core, pa)

    other_core = ((x * NZ + z) * NC + (1 - core), pa)

    loads = []
    for half in range(2):
        cols = slice(half * (D // 2), (half + 1) * (D // 2))
        for i, (source, first, count) in enumerate(
                ((q_hbm, 0, ROWS), (b_hbm, ROWS, BANK), (p_hbm, ROWS + BANK, SHARE))):
            loads.append(pltpu.make_async_copy(
                source.at[:, cols], rows.at[first:first + count, cols], load_sem.at[half, i]))
    load_neg = pltpu.make_async_copy(neg_hbm, neg, load_sem.at[0, 3])
    for load in loads:
        load.start()
    load_neg.start()

    barrier = pltpu.get_barrier_semaphore()
    partners = [at_y(step) for step in range(1, NY)] + [other_core, at_x(1), at_x(NX - 1)]
    for partner in partners:
        pl.semaphore_signal(barrier, inc=1, device_id=partner, device_id_type=MESH)

    @pl.when(z != HUB)
    def _():
        pl.semaphore_signal(barrier, inc=1, device_id=((x * NZ + HUB) * NC + core, pa), device_id_type=MESH)

    rows[ROWS + BANK + SHARE:2 * ROWS, :] = jnp.zeros((ROWS - BANK - SHARE, D), BF16)

    lane = iota((ROWS, ROWS), 1)
    sub = iota((ROWS, ROWS), 0)
    eye = lane == sub

    def pick(mask, values, axis):
        return jnp.sum(jnp.where(mask, values, 0.0), axis=axis, keepdims=True)

    gram_left, gram_c = 0.0, 0.0
    for half in range(2):
        for load in loads[3 * half:3 * half + 3]:
            load.wait()
        cols = slice(half * (D // 2), (half + 1) * (D // 2))
        gram_left = gram_left + nt(rows[:, cols], rows[:ROWS, cols])
        gram_c = gram_c + nt(rows[ROWS:, cols], rows[ROWS:, cols])
    gram_q, raw = gram_left[:ROWS], gram_left[ROWS:]
    load_neg.wait()
    q_scale_row = lax.rsqrt(pick(eye, gram_q, 0) + EPSILON)
    c_scale_col = lax.rsqrt(pick(eye, gram_c, 1) + EPSILON)
    c_scale_row = lax.rsqrt(pick(eye, gram_c, 0) + EPSILON)
    scores = raw * c_scale_col * (q_scale_row * INVERSE)
    ids = jnp.where(sub < BANK, sub + pa * BANK, -1)
    counts = jnp.where((sub >= BANK) & (sub < BANK + SHARE), 1.0, 0.0)
    for k in range(NEG):
        counts = counts + jnp.where(neg[k:k + 1, :] == ids, 1.0, 0.0)
    exps_t = jnp.exp(scores) * counts
    total_part[...] = jnp.broadcast_to(jnp.sum(exps_t, axis=0, keepdims=True), (8, ROWS))
    totals[pl.ds(pa, 1)] = total_part[...][None]

    pl.semaphore_wait(barrier, len(partners) + jnp.where(z == HUB, NZ - 1, 0))

    @pl.when(z == HUB)
    def _():
        for step in range(1, NZ):
            pl.semaphore_signal(all_here, inc=1, device_id=at_z(step), device_id_type=MESH)


    for place in range(NY - 1):
        pltpu.make_async_remote_copy(
            src_ref=total_part, dst_ref=totals.at[pa],
            send_sem=t_send_sem, recv_sem=t_recv_sem,
            device_id=(pb, place + jnp.where(place >= pa, 1, 0)), device_id_type=MESH).start()

    weight = jnp.transpose(exps_t * c_scale_col).astype(BF16)

    def part_piece(piece):
        for block in range(PIECE // 256):
            cols = pl.ds(piece * PIECE + block * 256, 256)
            part[:, cols] = jnp.dot(weight, rows[ROWS:, cols], preferred_element_type=F32)

    def y_rows(step):
        return pl.ds(pl.multiple_of(((pa + step) % NY) * SHARE, SHARE), SHARE)

    def y_distance(m):
        return 4 - (m + 1) // 2

    def y_pieces(s, m):
        half = s if m % 2 == 0 else 1 - s
        return (2 * half, 2 * half + 1)

    y_copies = []

    def y_copy(s, m, j):
        sign = 1 if s == 0 else -1
        piece = y_pieces(s, m)[j]
        return pltpu.make_async_remote_copy(
            src_ref=part.at[y_rows((sign * y_distance(m)) % NY), pl.ds(piece * PIECE, PIECE)],
            dst_ref=y_recv.at[s, m, j],
            send_sem=y_send_sem.at[s, m, j], recv_sem=y_recv_sem.at[s, m, j],
            device_id=at_y(sign % NY), device_id_type=MESH)

    def y_send(s, m, j):
        copy = y_copy(s, m, j)
        copy.start()
        y_copies.append(copy)

    part_piece(0)
    y_send(0, 0, 0)
    part_piece(2)
    y_send(1, 0, 0)
    part_piece(1)
    y_send(0, 0, 1)
    part_piece(3)
    y_send(1, 0, 1)
    for j in range(2):
        for s in range(2):
            y_send(s, 1, j)

    def y_step(m, j):
        for s in range(2):
            y_copy(s, m, j).wait_recv()
            sign = 1 if s == 0 else -1
            dest = y_rows((sign * (y_distance(m) - 1)) % NY)
            cols = pl.ds(y_pieces(s, m)[j] * PIECE, PIECE)
            part[dest, cols] = part[dest, cols] + y_recv[s, m, j]
            y_send(s, m + 2, j)

    order = jnp.where(sub < BANK, (sub % HALF_ROWS) * NC + sub // HALF_ROWS, sub)
    move = jnp.where(lane == order, 1.0, 0.0).astype(BF16)
    high = exps_t.astype(BF16)
    rest = exps_t - high.astype(F32)
    middle = rest.astype(BF16)
    low = (rest - middle.astype(F32)).astype(BF16)
    ordered = (jnp.dot(move, high, preferred_element_type=F32)
               + jnp.dot(move, middle, preferred_element_type=F32)
               + jnp.dot(move, low, preferred_element_type=F32))

    pltpu.make_async_copy(totals.at[1:NY], totals.at[1:NY], t_recv_sem).wait()
    total_row = jnp.sum(totals[...], axis=0)[0:1, :]
    weight_t = (ordered * (q_scale_row * INVERSE / total_row)).astype(BF16)

    c_copies, x_copies = [], []

    def core_rows(which):
        return pl.ds(pl.multiple_of(which * (HALF_ROWS * SUB), HALF_ROWS * SUB), HALF_ROWS * SUB)

    for piece in range(NT):
        for block in range(THIN // 256):
            cols = pl.ds(piece * THIN + block * 256, 256)
            product = jnp.dot(weight_t, rows[0:ROWS, cols], preferred_element_type=F32)
            passage_up[:, cols] = product[BANK:BANK + SHARE, :]
            for r in range(BANK // 8):
                for c in range(2):
                    bank[piece, pl.ds(r * 8 * SUB + block * 2 + c, 8, stride=SUB), :] = (
                        product[r * 8:r * 8 + 8, c * 128:c * 128 + 128])
        copy = pltpu.make_async_remote_copy(
            src_ref=bank.at[piece, core_rows(1 - core)], dst_ref=c_recv.at[piece],
            send_sem=c_send_sem.at[piece], recv_sem=c_recv_sem.at[piece],
            device_id=other_core, device_id_type=MESH)
        copy.start()
        c_copies.append(copy)

    def x_rows(step):
        start = core * (HALF_ROWS * SUB) + ((x + step) % NX) * (CHUNK * SUB)
        return pl.ds(pl.multiple_of(start, CHUNK * SUB), CHUNK * SUB)

    def x_copy(stage, piece, s):
        sign = 1 if s == 0 else -1
        recv = x_recv1.at[piece] if stage == 1 else x_recv2.at[piece, s]
        send_sem = x1_send_sem.at[piece] if stage == 1 else x2_send_sem.at[piece, s]
        recv_sem = x1_recv_sem.at[piece] if stage == 1 else x2_recv_sem.at[piece, s]
        return pltpu.make_async_remote_copy(
            src_ref=bank.at[piece, x_rows(2 if stage == 1 else sign % NX)], dst_ref=recv,
            send_sem=send_sem, recv_sem=recv_sem,
            device_id=at_x(sign % NX), device_id_type=MESH)

    def x_send(stage, piece, s):
        copy = x_copy(stage, piece, s)
        copy.start()
        x_copies.append(copy)

    def c_step(batch):
        for piece in (2 * batch, 2 * batch + 1):
            c_copies[piece].wait_recv()
            own = core_rows(core)
            bank[piece, own, :] = bank[piece, own, :] + c_recv[piece]

    def x_first(batch, stage):
        for s in range(2):
            x_send(stage, 2 * batch + (s if stage == 1 else 1 - s), s)

    def x1_step(batch):
        for s in range(2):
            piece = 2 * batch + s
            sign = 1 if s == 0 else -1
            x_copy(1, piece, s).wait_recv()
            dest = x_rows(sign % NX)
            bank[piece, dest, :] = bank[piece, dest, :] + x_recv1[piece]
            x_send(2, piece, s)

    def x2_step(batch):
        for s in range(2):
            piece = 2 * batch + s
            for t in range(2):
                x_copy(2, piece, t).wait_recv()
            total = bank[piece, x_rows(0), :] + x_recv2[piece, 0] + x_recv2[piece, 1]
            z_send[batch, :, s * SUB:(s + 1) * SUB, :] = total.reshape(CHUNK, SUB, 128)
        for place in range(NZ - 1):
            target = place + jnp.where(place >= z, 1, 0)
            pltpu.make_async_remote_copy(
                src_ref=z_send.at[batch, target], dst_ref=z_recv.at[batch, z],
                send_sem=z_send_sem.at[batch], recv_sem=z_recv_sem.at[batch],
                device_id=((x * NZ + target) * NC + core, pa), device_id_type=MESH).start()
        z_recv[batch, pl.ds(z, 1)] = z_send[batch, pl.ds(z, 1)]

    def z_step(batch):
        rest = z_recv.at[batch, 1:NZ]
        pltpu.make_async_copy(rest, rest, z_recv_sem.at[batch]).wait()
        return jnp.sum(z_recv[batch], axis=0)

    def norm_back(wide, scale, upstream):
        inner = jnp.sum(wide * upstream, axis=1, keepdims=True)
        return scale * upstream - (scale * scale * scale * inner) * wide

    own_lane, own_sub = iota((SHARE, ROWS), 1), iota((SHARE, ROWS), 0)
    own_query = own_lane == own_sub + pa * SHARE
    q_scale_own = pick(own_query, q_scale_row, 1)
    total_own = pick(own_query, total_row, 1)
    p_scale_own = pick(own_lane == own_sub + BANK, c_scale_row, 1)

    for batch in range(NB):
        c_step(batch)
        x_first(batch, 1)
        if batch < 2:
            x_first(batch, 2)
    y_step(0, 0)
    x1_step(0)
    x_first(2, 2)
    y_step(0, 1)
    x1_step(1)
    x_first(3, 2)

    @pl.when(z != HUB)
    def _():
        pl.semaphore_wait(all_here, 1)

    x2_step(0)
    y_step(1, 0)
    x1_step(2)
    x2_step(1)
    y_step(1, 1)
    x1_step(3)
    x2_step(2)
    y_step(2, 0)
    x2_step(3)

    own_q_rows = pl.ds(pl.multiple_of(pa * SHARE, SHARE), SHARE)
    own_q = rows[own_q_rows, :].astype(F32)
    own_p = rows[ROWS + BANK:ROWS + BANK + SHARE, :].astype(F32)
    passage_v = passage_up[...] - own_q * (q_scale_own * INVERSE)
    out_p[...] = norm_back(own_p, p_scale_own, passage_v)
    store_p = pltpu.make_async_copy(out_p, pg_hbm, store_sem.at[0])
    store_p.start()
    own_score = pick(own_query, scores[BANK:BANK + SHARE, :], 1)
    loss = pick(own_lane == own_sub, jnp.log(total_own) - own_score, 0)
    out_loss[...] = loss[:, :SHARE]
    store_loss = pltpu.make_async_copy(out_loss, loss_hbm, store_sem.at[1])
    store_loss.start()

    y_step(2, 1)

    one_hot = jnp.where(iota((SHARE, ROWS), 1) == pb, 1.0, 0.0).astype(BF16)
    for block in range(D // 256):
        row = jnp.dot(one_hot, rows[ROWS:, block * 256:block * 256 + 256], preferred_element_type=F32)
        for c in range(2):
            own_row[block * 2 + c:block * 2 + c + 1, :] = row[0:1, c * 128:c * 128 + 128]

    y_step(3, 0)
    y_step(3, 1)
    y_step(4, 0)
    y_step(4, 1)

    inverse_own = INVERSE / total_own
    own = y_rows(0)
    inner = jnp.zeros((SHARE, 1), F32)
    for m in (5, 6):
        for j in range(2):
            for s in range(2):
                y_copy(s, m, j).wait_recv()
    for piece in range(D // PIECE):
        half, j = piece // 2, piece % 2
        cols = pl.ds(piece * PIECE, PIECE)
        arrived = y_recv[0, 6 if half == 0 else 5, j] + y_recv[1, 5 if half == 0 else 6, j]
        value = (part[own, cols] + arrived) * inverse_own
        value = value - own_p[:, piece * PIECE:(piece + 1) * PIECE] * (p_scale_own * INVERSE)
        out_q[:, cols] = value
        inner = inner + jnp.sum(value * own_q[:, piece * PIECE:(piece + 1) * PIECE], axis=1, keepdims=True)
    out_q[...] = q_scale_own * out_q[...] - (q_scale_own * q_scale_own * q_scale_own * inner) * own_q
    store_q = pltpu.make_async_copy(out_q, qg_hbm, store_sem.at[3])
    store_q.start()

    def whole(values):
        return jnp.sum(jnp.sum(values, axis=0, keepdims=True), axis=1, keepdims=True)

    wide = own_row[...]
    scale = lax.rsqrt(whole(wide * wide) + EPSILON)
    for copy in y_copies + c_copies + x_copies:
        copy.wait_send()
    pltpu.make_async_copy(totals.at[1:NY], totals.at[1:NY], t_send_sem).wait()
    for batch in range(NB):
        rest = z_send.at[batch, 1:NZ]
        pltpu.make_async_copy(rest, rest, z_send_sem.at[batch]).wait()
    for store in (store_p, store_loss, store_q):
        store.wait()

    bank_v = jnp.concatenate([z_step(batch) for batch in range(NB)], axis=0)
    out_b[...] = scale * bank_v - (scale * scale * scale * whole(wide * bank_v)) * wide
    store_b = pltpu.make_async_copy(out_b, bg_hbm, store_sem.at[2])
    store_b.start()
    store_b.wait()


def hand_over(*refs):
    copies = [pltpu.make_async_copy(refs[i], refs[4 + i], refs[8].at[i]) for i in range(4)]
    for copy in copies:
        copy.start()
    for copy in copies:
        copy.wait()


def on_device(queries, positives, negative_pool, negatives):
    anywhere = pl.BlockSpec(memory_space=pl.ANY)
    dma = pltpu.SemaphoreType.DMA
    query_grad, positive_grad, pool_grad, losses = pl.pallas_call(
        kernel,
        out_shape=(
            jax.ShapeDtypeStruct((SHARE, D), F32),
            jax.ShapeDtypeStruct((SHARE, D), F32),
            jax.ShapeDtypeStruct((D // 128, 128), F32),
            jax.ShapeDtypeStruct((1, SHARE), F32),
        ),
        in_specs=[anywhere] * 4,
        out_specs=(anywhere,) * 4,
        scratch_shapes=[
            pltpu.VMEM((2 * ROWS, D), BF16),
            pltpu.VMEM((NEG, ROWS), jnp.int32),
            pltpu.VMEM((ROWS, D), F32),
            pltpu.VMEM((D // 128, 128), F32),
            pltpu.VMEM((SHARE, D), F32),
            pltpu.VMEM((SHARE, D), F32),
            pltpu.VMEM((SHARE, D), F32),
            pltpu.VMEM((D // 128, 128), F32),
            pltpu.VMEM((1, SHARE), F32),
            pltpu.VMEM((NY, 8, ROWS), F32),
            pltpu.VMEM((8, ROWS), F32),
            pltpu.VMEM((2, 7, 2, SHARE, PIECE), F32),
            pltpu.VMEM((NT, BANK * SUB, 128), F32),
            pltpu.VMEM((NT, HALF_ROWS * SUB, 128), F32),
            pltpu.VMEM((NT, CHUNK * SUB, 128), F32),
            pltpu.VMEM((NT, 2, CHUNK * SUB, 128), F32),
            pltpu.VMEM((NB, CHUNK, 2 * SUB, 128), F32),
            pltpu.VMEM((NB, CHUNK, 2 * SUB, 128), F32),
            dma((2, 4)), dma((4,)), dma, dma,
            dma((2, 7, 2)), dma((2, 7, 2)),
            dma((NT,)), dma((NT,)), dma((NT,)), dma((NT,)),
            dma((NT, 2)), dma((NT, 2)), dma((NB,)), dma((NB,)), pltpu.SemaphoreType.REGULAR,
        ],
        compiler_params=pltpu.CompilerParams(
            collective_id=0, has_side_effects=True, vmem_limit_bytes=40 * 1024 * 1024),
    )(*[pltpu.with_memory_space_constraint(t, pltpu.HBM) for t in (queries, positives, negative_pool, negatives.T)])
    query_grad, positive_grad, pool_grad, losses = pl.pallas_call(
        hand_over,
        out_shape=(
            jax.ShapeDtypeStruct((SHARE, D), F32),
            jax.ShapeDtypeStruct((SHARE, D), F32),
            jax.ShapeDtypeStruct((D // 128, 128), F32),
            jax.ShapeDtypeStruct((1, SHARE), F32),
        ),
        in_specs=[anywhere] * 4,
        out_specs=(anywhere,) * 4,
        scratch_shapes=[dma((4,))],
        compiler_params=pltpu.CompilerParams(vmem_limit_bytes=4 * 1024 * 1024),
    )(query_grad, positive_grad, pool_grad, losses)
    return query_grad, positive_grad, pool_grad.reshape(1, 1, D), losses.reshape(SHARE)


def solution(mesh):
    placed = (P("pb", None), P(("pb", "pa"), None), P("pa", None), P("pb", None))
    return jax.shard_map(
        on_device,
        mesh=mesh,
        in_specs=placed,
        out_specs=(
            P(("pb", "pa"), None),
            P(("pb", "pa"), None),
            P("pa", "pb", None),
            P(("pb", "pa")),
        ),
        check_vma=False,
    )
```

```python
import functools

import jax
import jax.numpy as jnp
from jax import lax
from jax.experimental import pallas as pl
from jax.experimental.pallas import tpu as pltpu
from jax.sharding import PartitionSpec as P

TEMPER = 0.02
INVERSE = 1.0 / TEMPER
EPSILON = 1e-06
NY, NX, NZ, NC = 8, 4, 12, 2
D = 4096
ROWS = 128
SHARE = 16
BANK = 96
NEG = 7
HALF = D // 2
THIN = 512
NT = D // THIN
HUB = 9
NB = NT // 2
SUB = THIN // 128
HALF_ROWS = BANK // NC
CHUNK = HALF_ROWS // NX
F32 = jnp.float32
BF16 = jnp.bfloat16
MESH = pl.DeviceIdType.MESH


def nt(left, right):
    return lax.dot_general(left, right, (((1,), (1,)), ((), ())), preferred_element_type=F32)


def iota(shape, dimension):
    return lax.broadcasted_iota(jnp.int32, shape, dimension)


def kernel(
    q_hbm, p_hbm, b_hbm, neg_hbm,
    qg_hbm, pg_hbm, bg_hbm, loss_hbm,
    rows, neg, part, own_row, passage_up, out_q, out_p, out_b, out_loss,
    totals, total_part, y_recv, bank, c_recv, x_recv1, x_recv2, z_send, z_recv,
    load_sem, store_sem, t_send_sem, t_recv_sem, y_send_sem, y_recv_sem,
    c_send_sem, c_recv_sem, x_send_sem, x1_recv_sem, x2_recv_sem,
    z_send_sem, z_recv_sem, all_here,
):
    pb, pa = lax.axis_index("pb"), lax.axis_index("pa")
    core, z, x = pb % NC, (pb // NC) % NZ, pb // (NC * NZ)

    def at_y(step):
        return (pb, (pa + step) % NY)

    def at_x(step):
        return ((((x + step) % NX) * NZ + z) * NC + core, pa)

    def at_z(step):
        return ((x * NZ + (z + step) % NZ) * NC + core, pa)

    other_core = ((x * NZ + z) * NC + (1 - core), pa)

    loads = [
        pltpu.make_async_copy(q_hbm, rows.at[0:ROWS], load_sem.at[0]),
        pltpu.make_async_copy(b_hbm, rows.at[ROWS:ROWS + BANK], load_sem.at[0]),
        pltpu.make_async_copy(p_hbm, rows.at[ROWS + BANK:ROWS + BANK + SHARE], load_sem.at[0]),
        pltpu.make_async_copy(neg_hbm, neg, load_sem.at[1]),
    ]
    for load in loads:
        load.start()

    barrier = pltpu.get_barrier_semaphore()
    partners = [at_y(step) for step in range(1, NY)] + [other_core, at_x(1), at_x(NX - 1)]
    for partner in partners:
        pl.semaphore_signal(barrier, inc=1, device_id=partner, device_id_type=MESH)

    @pl.when(z != HUB)
    def _():
        pl.semaphore_signal(barrier, inc=1, device_id=((x * NZ + HUB) * NC + core, pa), device_id_type=MESH)

    rows[ROWS + BANK + SHARE:2 * ROWS, :] = jnp.zeros((ROWS - BANK - SHARE, D), BF16)

    def arrive(like, sem):
        pltpu.make_async_copy(like, like, sem).wait()

    lane = iota((ROWS, ROWS), 1)
    sub = iota((ROWS, ROWS), 0)
    eye = lane == sub

    def pick(mask, values, axis):
        return jnp.sum(jnp.where(mask, values, 0.0), axis=axis, keepdims=True)

    arrive(rows.at[0:ROWS + BANK + SHARE], load_sem.at[0])
    gram = nt(rows[...], rows[...])
    gram_q, raw, gram_c = gram[:ROWS, :ROWS], gram[ROWS:, :ROWS], gram[ROWS:, ROWS:]
    loads[3].wait()
    q_scale_row = lax.rsqrt(pick(eye, gram_q, 0) + EPSILON)
    c_scale_col = lax.rsqrt(pick(eye, gram_c, 1) + EPSILON)
    c_scale_row = lax.rsqrt(pick(eye, gram_c, 0) + EPSILON)
    scores = raw * c_scale_col * (q_scale_row * INVERSE)
    ids = jnp.where(sub < BANK, sub + pa * BANK, -1)
    counts = jnp.where((sub >= BANK) & (sub < BANK + SHARE), 1.0, 0.0)
    for k in range(NEG):
        counts = counts + jnp.where(neg[k:k + 1, :] == ids, 1.0, 0.0)
    exps_t = jnp.exp(scores) * counts
    total_part[...] = jnp.broadcast_to(jnp.sum(exps_t, axis=0, keepdims=True), (8, ROWS))
    totals[pl.ds(pa, 1)] = total_part[...][None]

    pl.semaphore_wait(barrier, len(partners) + jnp.where(z == HUB, NZ - 1, 0))

    @pl.when(z == HUB)
    def _():
        for step in range(1, NZ):
            pl.semaphore_signal(all_here, inc=1, device_id=at_z(step), device_id_type=MESH)


    for place in range(NY - 1):
        pltpu.make_async_remote_copy(
            src_ref=total_part, dst_ref=totals.at[pa],
            send_sem=t_send_sem, recv_sem=t_recv_sem,
            device_id=(pb, place + jnp.where(place >= pa, 1, 0)), device_id_type=MESH).start()

    weight = jnp.transpose(exps_t * c_scale_col).astype(BF16)

    def part_half(half):
        for block in range(HALF // 256):
            cols = pl.ds(half * HALF + block * 256, 256)
            part[:, cols] = jnp.dot(weight, rows[ROWS:, cols], preferred_element_type=F32)

    def y_rows(step):
        return pl.ds(pl.multiple_of(((pa + step) % NY) * SHARE, SHARE), SHARE)

    def y_distance(m):
        return 4 - (m + 1) // 2

    def y_half(s, m):
        return s if m % 2 == 0 else 1 - s

    def y_copy(s, m):
        sign = 1 if s == 0 else -1
        return pltpu.make_async_remote_copy(
            src_ref=part.at[y_rows((sign * y_distance(m)) % NY), pl.ds(y_half(s, m) * HALF, HALF)],
            dst_ref=y_recv.at[s, m],
            send_sem=y_send_sem, recv_sem=y_recv_sem.at[s, m],
            device_id=at_y(sign % NY), device_id_type=MESH)

    for s in range(2):
        part_half(s)
        y_copy(s, 0).start()
    for s in range(2):
        y_copy(s, 1).start()

    def y_step(m):
        for s in range(2):
            y_copy(s, m).wait_recv()
            sign = 1 if s == 0 else -1
            dest = y_rows((sign * (y_distance(m) - 1)) % NY)
            cols = pl.ds(y_half(s, m) * HALF, HALF)
            part[dest, cols] = part[dest, cols] + y_recv[s, m]
            y_copy(s, m + 2).start()

    order = jnp.where(sub < BANK, (sub % HALF_ROWS) * NC + sub // HALF_ROWS, sub)
    move = jnp.where(lane == order, 1.0, 0.0).astype(BF16)
    high = exps_t.astype(BF16)
    rest = exps_t - high.astype(F32)
    middle = rest.astype(BF16)
    low = (rest - middle.astype(F32)).astype(BF16)
    ordered = (jnp.dot(move, high, preferred_element_type=F32)
               + jnp.dot(move, middle, preferred_element_type=F32)
               + jnp.dot(move, low, preferred_element_type=F32))

    arrive(totals.at[1:NY], t_recv_sem)
    total_row = jnp.sum(totals[...], axis=0)[0:1, :]
    weight_t = (ordered * (q_scale_row * INVERSE / total_row)).astype(BF16)

    def core_rows(which):
        return pl.ds(pl.multiple_of(which * (HALF_ROWS * SUB), HALF_ROWS * SUB), HALF_ROWS * SUB)

    for piece in range(NT):
        for block in range(THIN // 256):
            cols = pl.ds(piece * THIN + block * 256, 256)
            product = jnp.dot(weight_t, rows[0:ROWS, cols], preferred_element_type=F32)
            passage_up[:, cols] = product[BANK:BANK + SHARE, :]
            for r in range(BANK // 8):
                for c in range(2):
                    bank[piece, pl.ds(r * 8 * SUB + block * 2 + c, 8, stride=SUB), :] = (
                        product[r * 8:r * 8 + 8, c * 128:c * 128 + 128])
        pltpu.make_async_remote_copy(
            src_ref=bank.at[piece, core_rows(1 - core)], dst_ref=c_recv.at[piece],
            send_sem=c_send_sem, recv_sem=c_recv_sem.at[piece // 2],
            device_id=other_core, device_id_type=MESH).start()

    def x_rows(step):
        start = core * (HALF_ROWS * SUB) + ((x + step) % NX) * (CHUNK * SUB)
        return pl.ds(pl.multiple_of(start, CHUNK * SUB), CHUNK * SUB)

    def x_send(stage, piece, s):
        sign = 1 if s == 0 else -1
        recv_sem = x1_recv_sem if stage == 1 else x2_recv_sem
        pltpu.make_async_remote_copy(
            src_ref=bank.at[piece, x_rows(2 if stage == 1 else sign % NX)],
            dst_ref=x_recv1.at[piece] if stage == 1 else x_recv2.at[piece, s],
            send_sem=x_send_sem.at[stage - 1], recv_sem=recv_sem.at[piece // 2],
            device_id=at_x(sign % NX), device_id_type=MESH).start()

    def c_step(batch):
        arrive(c_recv.at[2 * batch:2 * batch + 2], c_recv_sem.at[batch])
        own = core_rows(core)
        for piece in (2 * batch, 2 * batch + 1):
            bank[piece, own, :] = bank[piece, own, :] + c_recv[piece]

    def x_first(batch, stage):
        for s in range(2):
            x_send(stage, 2 * batch + (s if stage == 1 else 1 - s), s)

    def x1_step(batch):
        arrive(x_recv1.at[2 * batch:2 * batch + 2], x1_recv_sem.at[batch])
        for s in range(2):
            piece = 2 * batch + s
            dest = x_rows((1 if s == 0 else -1) % NX)
            bank[piece, dest, :] = bank[piece, dest, :] + x_recv1[piece]
            x_send(2, piece, s)

    def x2_step(batch):
        arrive(x_recv2.at[2 * batch:2 * batch + 2], x2_recv_sem.at[batch])
        for s in range(2):
            piece = 2 * batch + s
            total = bank[piece, x_rows(0), :] + x_recv2[piece, 0] + x_recv2[piece, 1]
            z_send[batch, :, s * SUB:(s + 1) * SUB, :] = total.reshape(CHUNK, SUB, 128)
        for place in range(NZ - 1):
            target = place + jnp.where(place >= z, 1, 0)
            pltpu.make_async_remote_copy(
                src_ref=z_send.at[batch, target], dst_ref=z_recv.at[batch, z],
                send_sem=z_send_sem, recv_sem=z_recv_sem,
                device_id=((x * NZ + target) * NC + core, pa), device_id_type=MESH).start()
        z_recv[batch, pl.ds(z, 1)] = z_send[batch, pl.ds(z, 1)]

    def norm_back(wide, scale, upstream):
        inner = jnp.sum(wide * upstream, axis=1, keepdims=True)
        return scale * upstream - (scale * scale * scale * inner) * wide

    own_lane, own_sub = iota((SHARE, ROWS), 1), iota((SHARE, ROWS), 0)
    own_query = own_lane == own_sub + pa * SHARE
    q_scale_own = pick(own_query, q_scale_row, 1)
    total_own = pick(own_query, total_row, 1)
    p_scale_own = pick(own_lane == own_sub + BANK, c_scale_row, 1)

    for batch in range(NB):
        c_step(batch)
        x_first(batch, 1)
    arrive(x_recv1, x_send_sem.at[0])
    for batch in range(NB):
        x_first(batch, 2)
    for batch in range(NB):
        x1_step(batch)
    y_step(0)

    @pl.when(z != HUB)
    def _():
        pl.semaphore_wait(all_here, 1)

    for batch in range(NB):
        x2_step(batch)
        if batch == 1:
            y_step(1)

    own_q_rows = pl.ds(pl.multiple_of(pa * SHARE, SHARE), SHARE)
    own_q = rows[own_q_rows, :].astype(F32)
    own_p = rows[ROWS + BANK:ROWS + BANK + SHARE, :].astype(F32)
    passage_v = passage_up[...] - own_q * (q_scale_own * INVERSE)
    out_p[...] = norm_back(own_p, p_scale_own, passage_v)
    store_p = pltpu.make_async_copy(out_p, pg_hbm, store_sem.at[0])
    store_p.start()
    own_score = pick(own_query, scores[BANK:BANK + SHARE, :], 1)
    loss = pick(own_lane == own_sub, jnp.log(total_own) - own_score, 0)
    out_loss[...] = loss[:, :SHARE]
    store_loss = pltpu.make_async_copy(out_loss, loss_hbm, store_sem.at[1])
    store_loss.start()

    y_step(2)

    one_hot = jnp.where(iota((SHARE, ROWS), 1) == pb, 1.0, 0.0).astype(BF16)
    for block in range(D // 256):
        row = jnp.dot(one_hot, rows[ROWS:, block * 256:block * 256 + 256], preferred_element_type=F32)
        for c in range(2):
            own_row[block * 2 + c:block * 2 + c + 1, :] = row[0:1, c * 128:c * 128 + 128]

    y_step(3)
    y_step(4)

    inverse_own = INVERSE / total_own
    own = y_rows(0)
    inner = jnp.zeros((SHARE, 1), F32)
    for m in (5, 6):
        for s in range(2):
            y_copy(s, m).wait_recv()
    for half in range(2):
        cols = slice(half * HALF, (half + 1) * HALF)
        arrived = y_recv[0, 6 if half == 0 else 5] + y_recv[1, 5 if half == 0 else 6]
        value = (part[own, cols] + arrived) * inverse_own
        value = value - own_p[:, cols] * (p_scale_own * INVERSE)
        out_q[:, cols] = value
        inner = inner + jnp.sum(value * own_q[:, cols], axis=1, keepdims=True)
    out_q[...] = q_scale_own * out_q[...] - (q_scale_own * q_scale_own * q_scale_own * inner) * own_q
    store_q = pltpu.make_async_copy(out_q, qg_hbm, store_sem.at[3])
    store_q.start()

    def whole(values):
        return jnp.sum(jnp.sum(values, axis=0, keepdims=True), axis=1, keepdims=True)

    wide = own_row[...]
    scale = lax.rsqrt(whole(wide * wide) + EPSILON)
    arrive(totals.at[1:NY], t_send_sem)
    arrive(y_recv, y_send_sem)
    arrive(c_recv, c_send_sem)
    arrive(x_recv2, x_send_sem.at[1])
    arrive(z_send.at[:, 1:NZ], z_send_sem)
    for store in (store_p, store_loss, store_q):
        store.wait()

    arrive(z_recv.at[:, 1:NZ], z_recv_sem)
    bank_v = jnp.sum(z_recv[...], axis=1).reshape(D // 128, 128)
    out_b[...] = scale * bank_v - (scale * scale * scale * whole(wide * bank_v)) * wide
    store_b = pltpu.make_async_copy(out_b, bg_hbm, store_sem.at[2])
    store_b.start()
    store_b.wait()


def hand_over(*refs):
    copies = [pltpu.make_async_copy(refs[i], refs[4 + i], refs[8].at[i]) for i in range(4)]
    for copy in copies:
        copy.start()
    for copy in copies:
        copy.wait()


def on_device(queries, positives, negative_pool, negatives):
    anywhere = pl.BlockSpec(memory_space=pl.ANY)
    dma = pltpu.SemaphoreType.DMA
    query_grad, positive_grad, pool_grad, losses = pl.pallas_call(
        kernel,
        out_shape=(
            jax.ShapeDtypeStruct((SHARE, D), F32),
            jax.ShapeDtypeStruct((SHARE, D), F32),
            jax.ShapeDtypeStruct((D // 128, 128), F32),
            jax.ShapeDtypeStruct((1, SHARE), F32),
        ),
        in_specs=[anywhere] * 4,
        out_specs=(anywhere,) * 4,
        scratch_shapes=[
            pltpu.VMEM((2 * ROWS, D), BF16),
            pltpu.VMEM((NEG, ROWS), jnp.int32),
            pltpu.VMEM((ROWS, D), F32),
            pltpu.VMEM((D // 128, 128), F32),
            pltpu.VMEM((SHARE, D), F32),
            pltpu.VMEM((SHARE, D), F32),
            pltpu.VMEM((SHARE, D), F32),
            pltpu.VMEM((D // 128, 128), F32),
            pltpu.VMEM((1, SHARE), F32),
            pltpu.VMEM((NY, 8, ROWS), F32),
            pltpu.VMEM((8, ROWS), F32),
            pltpu.VMEM((2, 7, SHARE, HALF), F32),
            pltpu.VMEM((NT, BANK * SUB, 128), F32),
            pltpu.VMEM((NT, HALF_ROWS * SUB, 128), F32),
            pltpu.VMEM((NT, CHUNK * SUB, 128), F32),
            pltpu.VMEM((NT, 2, CHUNK * SUB, 128), F32),
            pltpu.VMEM((NB, CHUNK, 2 * SUB, 128), F32),
            pltpu.VMEM((NB, CHUNK, 2 * SUB, 128), F32),
            dma((2,)), dma((4,)), dma, dma, dma, dma((2, 7)),
            dma, dma((NB,)), dma((2,)), dma((NB,)), dma((NB,)),
            dma, dma, pltpu.SemaphoreType.REGULAR,
        ],
        compiler_params=pltpu.CompilerParams(
            collective_id=0, has_side_effects=True, vmem_limit_bytes=40 * 1024 * 1024),
    )(*[pltpu.with_memory_space_constraint(t, pltpu.HBM) for t in (queries, positives, negative_pool, negatives.T)])
    query_grad, positive_grad, pool_grad, losses = pl.pallas_call(
        hand_over,
        out_shape=(
            jax.ShapeDtypeStruct((SHARE, D), F32),
            jax.ShapeDtypeStruct((SHARE, D), F32),
            jax.ShapeDtypeStruct((D // 128, 128), F32),
            jax.ShapeDtypeStruct((1, SHARE), F32),
        ),
        in_specs=[anywhere] * 4,
        out_specs=(anywhere,) * 4,
        scratch_shapes=[dma((4,))],
        compiler_params=pltpu.CompilerParams(vmem_limit_bytes=4 * 1024 * 1024),
    )(query_grad, positive_grad, pool_grad, losses)
    return query_grad, positive_grad, pool_grad.reshape(1, 1, D), losses.reshape(SHARE)


def solution(mesh):
    placed = (P("pb", None), P(("pb", "pa"), None), P("pa", None), P("pb", None))
    return jax.shard_map(
        on_device,
        mesh=mesh,
        in_specs=placed,
        out_specs=(
            P(("pb", "pa"), None),
            P(("pb", "pa"), None),
            P("pa", "pb", None),
            P(("pb", "pa")),
        ),
        check_vma=False,
    )
```

```python
import functools

import jax
import jax.numpy as jnp
from jax import lax
from jax.experimental import pallas as pl
from jax.experimental.pallas import tpu as pltpu
from jax.sharding import PartitionSpec as P

TEMPER = 0.02
INVERSE = 1.0 / TEMPER
EPSILON = 1e-06
NY, NX, NZ, NC = 8, 4, 12, 2
D = 4096
ROWS = 128
SHARE = 16
BANK = 96
NEG = 7
HALF = D // 2
SUB = HALF // 128
HUB = 9
NB = 4
GROUP = NZ // NB
BATCH_ROWS = BANK // NB
HALF_ROWS = BATCH_ROWS // NC
CHUNK = HALF_ROWS // NX
NT = 2 * NB
F32 = jnp.float32
BF16 = jnp.bfloat16
MESH = pl.DeviceIdType.MESH


def nt(left, right):
    return lax.dot_general(left, right, (((1,), (1,)), ((), ())), preferred_element_type=F32)


def iota(shape, dimension):
    return lax.broadcasted_iota(jnp.int32, shape, dimension)


def kernel(
    q_hbm, p_hbm, b_hbm, neg_hbm,
    qg_hbm, pg_hbm, bg_hbm, loss_hbm,
    rows, neg, part, own_row, passage_up, out_q, out_p, out_b, out_loss,
    totals, total_part, y_recv, bank, c_recv, x_recv1, x_recv2, z_send, z_recv,
    load_sem, store_sem, t_send_sem, t_recv_sem, y_send_sem, y_recv_sem,
    c_send_sem, c_recv_sem, x_send_sem, x1_recv_sem, x2_recv_sem,
    z_send_sem, z_recv_sem, all_here,
):
    pb, pa = lax.axis_index("pb"), lax.axis_index("pa")
    core, z, x = pb % NC, (pb // NC) % NZ, pb // (NC * NZ)

    def at_y(step):
        return (pb, (pa + step) % NY)

    def at_x(step):
        return ((((x + step) % NX) * NZ + z) * NC + core, pa)

    def at_z(step):
        return ((x * NZ + (z + step) % NZ) * NC + core, pa)

    other_core = ((x * NZ + z) * NC + (1 - core), pa)

    loads = [
        pltpu.make_async_copy(q_hbm, rows.at[0:ROWS], load_sem.at[0]),
        pltpu.make_async_copy(b_hbm, rows.at[ROWS:ROWS + BANK], load_sem.at[0]),
        pltpu.make_async_copy(p_hbm, rows.at[ROWS + BANK:ROWS + BANK + SHARE], load_sem.at[0]),
        pltpu.make_async_copy(neg_hbm, neg, load_sem.at[1]),
    ]
    for load in loads:
        load.start()

    barrier = pltpu.get_barrier_semaphore()
    partners = [at_y(step) for step in range(1, NY)] + [other_core, at_x(1), at_x(NX - 1)]
    for partner in partners:
        pl.semaphore_signal(barrier, inc=1, device_id=partner, device_id_type=MESH)

    @pl.when(z != HUB)
    def _():
        pl.semaphore_signal(barrier, inc=1, device_id=((x * NZ + HUB) * NC + core, pa), device_id_type=MESH)

    rows[ROWS + BANK + SHARE:2 * ROWS, :] = jnp.zeros((ROWS - BANK - SHARE, D), BF16)

    def arrive(like, sem):
        pltpu.make_async_copy(like, like, sem).wait()

    lane = iota((ROWS, ROWS), 1)
    sub = iota((ROWS, ROWS), 0)
    eye = lane == sub

    def pick(mask, values, axis):
        return jnp.sum(jnp.where(mask, values, 0.0), axis=axis, keepdims=True)

    arrive(rows.at[0:ROWS + BANK + SHARE], load_sem.at[0])
    gram = nt(rows[...], rows[...])
    gram_q, raw, gram_c = gram[:ROWS, :ROWS], gram[ROWS:, :ROWS], gram[ROWS:, ROWS:]
    loads[3].wait()
    q_scale_row = lax.rsqrt(pick(eye, gram_q, 0) + EPSILON)
    c_scale_col = lax.rsqrt(pick(eye, gram_c, 1) + EPSILON)
    c_scale_row = lax.rsqrt(pick(eye, gram_c, 0) + EPSILON)
    scores = raw * c_scale_col * (q_scale_row * INVERSE)
    ids = jnp.where(sub < BANK, sub + pa * BANK, -1)
    counts = jnp.where((sub >= BANK) & (sub < BANK + SHARE), 1.0, 0.0)
    for k in range(NEG):
        counts = counts + jnp.where(neg[k:k + 1, :] == ids, 1.0, 0.0)
    exps_t = jnp.exp(scores) * counts
    total_part[...] = jnp.broadcast_to(jnp.sum(exps_t, axis=0, keepdims=True), (8, ROWS))
    totals[pl.ds(pa, 1)] = total_part[...][None]

    pl.semaphore_wait(barrier, len(partners) + jnp.where(z == HUB, NZ - 1, 0))

    @pl.when(z == HUB)
    def _():
        for step in range(1, NZ):
            pl.semaphore_signal(all_here, inc=1, device_id=at_z(step), device_id_type=MESH)


    for place in range(NY - 1):
        pltpu.make_async_remote_copy(
            src_ref=total_part, dst_ref=totals.at[pa],
            send_sem=t_send_sem, recv_sem=t_recv_sem,
            device_id=(pb, place + jnp.where(place >= pa, 1, 0)), device_id_type=MESH).start()

    weight = jnp.transpose(exps_t * c_scale_col).astype(BF16)

    def part_half(half):
        for block in range(HALF // 256):
            cols = pl.ds(half * HALF + block * 256, 256)
            part[:, cols] = jnp.dot(weight, rows[ROWS:, cols], preferred_element_type=F32)

    def y_rows(step):
        return pl.ds(pl.multiple_of(((pa + step) % NY) * SHARE, SHARE), SHARE)

    def y_distance(m):
        return 4 - (m + 1) // 2

    def y_half(s, m):
        return s if m % 2 == 0 else 1 - s

    def y_copy(s, m):
        sign = 1 if s == 0 else -1
        return pltpu.make_async_remote_copy(
            src_ref=part.at[y_rows((sign * y_distance(m)) % NY), pl.ds(y_half(s, m) * HALF, HALF)],
            dst_ref=y_recv.at[s, m],
            send_sem=y_send_sem, recv_sem=y_recv_sem.at[s, m],
            device_id=at_y(sign % NY), device_id_type=MESH)

    for s in range(2):
        part_half(s)
        y_copy(s, 0).start()
    for s in range(2):
        y_copy(s, 1).start()

    def y_step(m):
        for s in range(2):
            y_copy(s, m).wait_recv()
            sign = 1 if s == 0 else -1
            dest = y_rows((sign * (y_distance(m) - 1)) % NY)
            cols = pl.ds(y_half(s, m) * HALF, HALF)
            part[dest, cols] = part[dest, cols] + y_recv[s, m]
            y_copy(s, m + 2).start()

    place = sub % BATCH_ROWS
    place_core, place_x, place_z = place // HALF_ROWS, (place % HALF_ROWS) // CHUNK, place % CHUNK
    bank_row = place_x * (NZ * NC) + ((sub // BATCH_ROWS) * GROUP + place_z) * NC + place_core
    order = jnp.where(sub < BANK, bank_row, sub)
    move = jnp.where(lane == order, 1.0, 0.0).astype(BF16)
    high = exps_t.astype(BF16)
    rest = exps_t - high.astype(F32)
    middle = rest.astype(BF16)
    low = (rest - middle.astype(F32)).astype(BF16)
    ordered = (jnp.dot(move, high, preferred_element_type=F32)
               + jnp.dot(move, middle, preferred_element_type=F32)
               + jnp.dot(move, low, preferred_element_type=F32))

    arrive(totals.at[1:NY], t_recv_sem)
    total_row = jnp.sum(totals[...], axis=0)[0:1, :]
    weight_t = (ordered * (q_scale_row * INVERSE / total_row)).astype(BF16)

    def core_rows(which):
        return pl.ds(pl.multiple_of(which * (HALF_ROWS * SUB), HALF_ROWS * SUB), HALF_ROWS * SUB)

    def c_copy(piece):
        return pltpu.make_async_remote_copy(
            src_ref=bank.at[piece, core_rows(1 - core)], dst_ref=c_recv.at[piece],
            send_sem=c_send_sem, recv_sem=c_recv_sem.at[piece // 2],
            device_id=other_core, device_id_type=MESH)

    for half in range(2):
        for block in range(HALF // 256):
            cols = pl.ds(half * HALF + block * 256, 256)
            product = jnp.dot(weight_t, rows[0:ROWS, cols], preferred_element_type=F32)
            passage_up[:, cols] = product[BANK:BANK + SHARE, :]
            for r in range(BANK // 8):
                batch, r8 = r // (BATCH_ROWS // 8), r % (BATCH_ROWS // 8)
                for c in range(2):
                    bank[2 * batch + half, pl.ds(r8 * 8 * SUB + block * 2 + c, 8, stride=SUB), :] = (
                        product[r * 8:r * 8 + 8, c * 128:c * 128 + 128])
        c_copy(half).start()
    for piece in range(2, NT):
        c_copy(piece).start()

    def x_rows(step):
        start = core * (HALF_ROWS * SUB) + ((x + step) % NX) * (CHUNK * SUB)
        return pl.ds(pl.multiple_of(start, CHUNK * SUB), CHUNK * SUB)

    def x_send(stage, piece, s):
        sign = 1 if s == 0 else -1
        recv_sem = x1_recv_sem if stage == 1 else x2_recv_sem
        pltpu.make_async_remote_copy(
            src_ref=bank.at[piece, x_rows(2 if stage == 1 else sign % NX)],
            dst_ref=x_recv1.at[piece] if stage == 1 else x_recv2.at[piece, s],
            send_sem=x_send_sem.at[stage - 1], recv_sem=recv_sem.at[piece // 2],
            device_id=at_x(sign % NX), device_id_type=MESH).start()

    def c_step(batch):
        arrive(c_recv.at[2 * batch:2 * batch + 2], c_recv_sem.at[batch])
        own = core_rows(core)
        for piece in (2 * batch, 2 * batch + 1):
            bank[piece, own, :] = bank[piece, own, :] + c_recv[piece]

    def x_first(batch, stage):
        for s in range(2):
            x_send(stage, 2 * batch + (s if stage == 1 else 1 - s), s)

    def x1_step(batch):
        arrive(x_recv1.at[2 * batch:2 * batch + 2], x1_recv_sem.at[batch])
        for s in range(2):
            piece = 2 * batch + s
            dest = x_rows((1 if s == 0 else -1) % NX)
            bank[piece, dest, :] = bank[piece, dest, :] + x_recv1[piece]
            x_send(2, piece, s)

    def x2_step(batch):
        arrive(x_recv2.at[2 * batch:2 * batch + 2], x2_recv_sem.at[batch])
        for s in range(2):
            piece = 2 * batch + s
            total = bank[piece, x_rows(0), :] + x_recv2[piece, 0] + x_recv2[piece, 1]
            z_send[batch * GROUP:(batch + 1) * GROUP, s * SUB:(s + 1) * SUB, :] = total.reshape(CHUNK, SUB, 128)
        for target in range(batch * GROUP, (batch + 1) * GROUP):
            @pl.when(z != target)
            def _():
                pltpu.make_async_remote_copy(
                    src_ref=z_send.at[target], dst_ref=z_recv.at[z],
                    send_sem=z_send_sem, recv_sem=z_recv_sem,
                    device_id=((x * NZ + target) * NC + core, pa), device_id_type=MESH).start()

    def norm_back(wide, scale, upstream):
        inner = jnp.sum(wide * upstream, axis=1, keepdims=True)
        return scale * upstream - (scale * scale * scale * inner) * wide

    own_lane, own_sub = iota((SHARE, ROWS), 1), iota((SHARE, ROWS), 0)
    own_query = own_lane == own_sub + pa * SHARE
    q_scale_own = pick(own_query, q_scale_row, 1)
    total_own = pick(own_query, total_row, 1)
    p_scale_own = pick(own_lane == own_sub + BANK, c_scale_row, 1)

    c_step(0)
    x_first(0, 1)
    x_first(0, 2)
    y_step(0)
    c_step(1)
    c_step(2)
    c_step(3)
    x1_step(0)
    x_first(1, 1)
    x_first(1, 2)
    x_first(2, 1)
    y_step(1)

    @pl.when(z != HUB)
    def _():
        pl.semaphore_wait(all_here, 1)

    x2_step(0)
    x1_step(1)
    x_first(2, 2)
    x_first(3, 1)
    y_step(2)
    x1_step(2)
    x_first(3, 2)
    x2_step(1)
    x1_step(3)
    y_step(3)
    x2_step(2)
    x2_step(3)
    z_recv[pl.ds(z, 1)] = z_send[pl.ds(z, 1)]

    own_q_rows = pl.ds(pl.multiple_of(pa * SHARE, SHARE), SHARE)
    own_q = rows[own_q_rows, :].astype(F32)
    own_p = rows[ROWS + BANK:ROWS + BANK + SHARE, :].astype(F32)
    passage_v = passage_up[...] - own_q * (q_scale_own * INVERSE)
    out_p[...] = norm_back(own_p, p_scale_own, passage_v)
    store_p = pltpu.make_async_copy(out_p, pg_hbm, store_sem.at[0])
    store_p.start()
    own_score = pick(own_query, scores[BANK:BANK + SHARE, :], 1)
    loss = pick(own_lane == own_sub, jnp.log(total_own) - own_score, 0)
    out_loss[...] = loss[:, :SHARE]
    store_loss = pltpu.make_async_copy(out_loss, loss_hbm, store_sem.at[1])
    store_loss.start()


    y_step(4)

    one_hot = jnp.where(iota((SHARE, ROWS), 1) == pb, 1.0, 0.0).astype(BF16)
    for block in range(D // 256):
        row = jnp.dot(one_hot, rows[ROWS:, block * 256:block * 256 + 256], preferred_element_type=F32)
        for c in range(2):
            own_row[block * 2 + c:block * 2 + c + 1, :] = row[0:1, c * 128:c * 128 + 128]


    inverse_own = INVERSE / total_own
    own = y_rows(0)
    inner = jnp.zeros((SHARE, 1), F32)
    for m in (5, 6):
        for s in range(2):
            y_copy(s, m).wait_recv()
    for half in range(2):
        cols = slice(half * HALF, (half + 1) * HALF)
        arrived = y_recv[0, 6 if half == 0 else 5] + y_recv[1, 5 if half == 0 else 6]
        value = (part[own, cols] + arrived) * inverse_own
        value = value - own_p[:, cols] * (p_scale_own * INVERSE)
        out_q[:, cols] = value
        inner = inner + jnp.sum(value * own_q[:, cols], axis=1, keepdims=True)
    out_q[...] = q_scale_own * out_q[...] - (q_scale_own * q_scale_own * q_scale_own * inner) * own_q
    store_q = pltpu.make_async_copy(out_q, qg_hbm, store_sem.at[3])
    store_q.start()

    def whole(values):
        return jnp.sum(jnp.sum(values, axis=0, keepdims=True), axis=1, keepdims=True)

    wide = own_row[...]
    scale = lax.rsqrt(whole(wide * wide) + EPSILON)
    arrive(totals.at[1:NY], t_send_sem)
    arrive(y_recv, y_send_sem)
    arrive(c_recv, c_send_sem)
    arrive(x_recv2, x_send_sem.at[1])
    arrive(z_send.at[1:NZ], z_send_sem)
    arrive(x_recv1, x_send_sem.at[0])
    for store in (store_p, store_loss, store_q):
        store.wait()

    arrive(z_recv.at[1:NZ], z_recv_sem)
    bank_v = jnp.sum(z_recv[...], axis=0)
    out_b[...] = scale * bank_v - (scale * scale * scale * whole(wide * bank_v)) * wide
    store_b = pltpu.make_async_copy(out_b, bg_hbm, store_sem.at[2])
    store_b.start()
    store_b.wait()


def hand_over(*refs):
    copies = [pltpu.make_async_copy(refs[i], refs[4 + i], refs[8].at[i]) for i in range(4)]
    for copy in copies:
        copy.start()
    for copy in copies:
        copy.wait()


def on_device(queries, positives, negative_pool, negatives):
    anywhere = pl.BlockSpec(memory_space=pl.ANY)
    dma = pltpu.SemaphoreType.DMA
    query_grad, positive_grad, pool_grad, losses = pl.pallas_call(
        kernel,
        out_shape=(
            jax.ShapeDtypeStruct((SHARE, D), F32),
            jax.ShapeDtypeStruct((SHARE, D), F32),
            jax.ShapeDtypeStruct((D // 128, 128), F32),
            jax.ShapeDtypeStruct((1, SHARE), F32),
        ),
        in_specs=[anywhere] * 4,
        out_specs=(anywhere,) * 4,
        scratch_shapes=[
            pltpu.VMEM((2 * ROWS, D), BF16),
            pltpu.VMEM((NEG, ROWS), jnp.int32),
            pltpu.VMEM((ROWS, D), F32),
            pltpu.VMEM((D // 128, 128), F32),
            pltpu.VMEM((SHARE, D), F32),
            pltpu.VMEM((SHARE, D), F32),
            pltpu.VMEM((SHARE, D), F32),
            pltpu.VMEM((D // 128, 128), F32),
            pltpu.VMEM((1, SHARE), F32),
            pltpu.VMEM((NY, 8, ROWS), F32),
            pltpu.VMEM((8, ROWS), F32),
            pltpu.VMEM((2, 7, SHARE, HALF), F32),
            pltpu.VMEM((NT, BATCH_ROWS * SUB, 128), F32),
            pltpu.VMEM((NT, HALF_ROWS * SUB, 128), F32),
            pltpu.VMEM((NT, CHUNK * SUB, 128), F32),
            pltpu.VMEM((NT, 2, CHUNK * SUB, 128), F32),
            pltpu.VMEM((NZ, D // 128, 128), F32),
            pltpu.VMEM((NZ, D // 128, 128), F32),
            dma((2,)), dma((4,)), dma, dma, dma, dma((2, 7)),
            dma, dma((NB,)), dma((2,)), dma((NB,)), dma((NB,)),
            dma, dma, pltpu.SemaphoreType.REGULAR,
        ],
        compiler_params=pltpu.CompilerParams(
            collective_id=0, has_side_effects=True, vmem_limit_bytes=40 * 1024 * 1024),
    )(*[pltpu.with_memory_space_constraint(t, pltpu.HBM) for t in (queries, positives, negative_pool, negatives.T)])
    query_grad, positive_grad, pool_grad, losses = pl.pallas_call(
        hand_over,
        out_shape=(
            jax.ShapeDtypeStruct((SHARE, D), F32),
            jax.ShapeDtypeStruct((SHARE, D), F32),
            jax.ShapeDtypeStruct((D // 128, 128), F32),
            jax.ShapeDtypeStruct((1, SHARE), F32),
        ),
        in_specs=[anywhere] * 4,
        out_specs=(anywhere,) * 4,
        scratch_shapes=[dma((4,))],
        compiler_params=pltpu.CompilerParams(vmem_limit_bytes=4 * 1024 * 1024),
    )(query_grad, positive_grad, pool_grad, losses)
    return query_grad, positive_grad, pool_grad.reshape(1, 1, D), losses.reshape(SHARE)


def solution(mesh):
    placed = (P("pb", None), P(("pb", "pa"), None), P("pa", None), P("pb", None))
    return jax.shard_map(
        on_device,
        mesh=mesh,
        in_specs=placed,
        out_specs=(
            P(("pb", "pa"), None),
            P(("pb", "pa"), None),
            P("pa", "pb", None),
            P(("pb", "pa")),
        ),
        check_vma=False,
    )
```

```python
import functools

import jax
import jax.numpy as jnp
from jax import lax
from jax.experimental import pallas as pl
from jax.experimental.pallas import tpu as pltpu
from jax.sharding import PartitionSpec as P

TEMPER = 0.02
INVERSE = 1.0 / TEMPER
EPSILON = 1e-06
NY, NX, NZ, NC = 8, 4, 12, 2
D = 4096
ROWS = 128
SHARE = 16
BANK = 96
NEG = 7
HALF = D // 2
SUB = HALF // 128
HUB = 9
NB = 4
GROUP = NZ // NB
BATCH_ROWS = BANK // NB
HALF_ROWS = BATCH_ROWS // NC
CHUNK = HALF_ROWS // NX
NT = 2 * NB
F32 = jnp.float32
BF16 = jnp.bfloat16
MESH = pl.DeviceIdType.MESH


def nt(left, right):
    return lax.dot_general(left, right, (((1,), (1,)), ((), ())), preferred_element_type=F32)


def iota(shape, dimension):
    return lax.broadcasted_iota(jnp.int32, shape, dimension)


def kernel(
    q_hbm, p_hbm, b_hbm, neg_hbm,
    qg_hbm, pg_hbm, bg_hbm, loss_hbm,
    rows, neg, part, own_row, passage_up, out_q, out_p, out_b, out_loss,
    totals, total_part, y_recv, bank, c_recv, x_recv1, x_recv2, z_send, z_recv,
    load_sem, store_sem, t_send_sem, t_recv_sem, y_send_sem, y_recv_sem,
    c_send_sem, c_recv_sem, x_send_sem, x1_recv_sem, x2_recv_sem,
    z_send_sem, z_recv_sem, all_here,
):
    pb, pa = lax.axis_index("pb"), lax.axis_index("pa")
    core, z, x = pb % NC, (pb // NC) % NZ, pb // (NC * NZ)

    def at_y(step):
        return (pb, (pa + step) % NY)

    def at_x(step):
        return ((((x + step) % NX) * NZ + z) * NC + core, pa)

    def at_z(step):
        return ((x * NZ + (z + step) % NZ) * NC + core, pa)

    other_core = ((x * NZ + z) * NC + (1 - core), pa)

    loads = [
        pltpu.make_async_copy(q_hbm, rows.at[0:ROWS], load_sem.at[0]),
        pltpu.make_async_copy(b_hbm, rows.at[ROWS:ROWS + BANK], load_sem.at[0]),
        pltpu.make_async_copy(p_hbm, rows.at[ROWS + BANK:ROWS + BANK + SHARE], load_sem.at[0]),
        pltpu.make_async_copy(neg_hbm, neg, load_sem.at[1]),
    ]
    for load in loads:
        load.start()

    barrier = pltpu.get_barrier_semaphore()
    partners = [at_y(step) for step in range(1, NY)] + [other_core, at_x(1), at_x(NX - 1)]
    for partner in partners:
        pl.semaphore_signal(barrier, inc=1, device_id=partner, device_id_type=MESH)

    @pl.when(z != HUB)
    def _():
        pl.semaphore_signal(barrier, inc=1, device_id=((x * NZ + HUB) * NC + core, pa), device_id_type=MESH)

    rows[ROWS + BANK + SHARE:2 * ROWS, :] = jnp.zeros((ROWS - BANK - SHARE, D), BF16)

    def arrive(like, sem):
        pltpu.make_async_copy(like, like, sem).wait()

    lane = iota((ROWS, ROWS), 1)
    sub = iota((ROWS, ROWS), 0)
    eye = lane == sub

    def pick(mask, values, axis):
        return jnp.sum(jnp.where(mask, values, 0.0), axis=axis, keepdims=True)

    arrive(rows.at[0:ROWS + BANK + SHARE], load_sem.at[0])
    gram = nt(rows[...], rows[...])
    gram_q, raw, gram_c = gram[:ROWS, :ROWS], gram[ROWS:, :ROWS], gram[ROWS:, ROWS:]
    loads[3].wait()
    q_scale_row = lax.rsqrt(pick(eye, gram_q, 0) + EPSILON)
    c_scale_col = lax.rsqrt(pick(eye, gram_c, 1) + EPSILON)
    c_scale_row = lax.rsqrt(pick(eye, gram_c, 0) + EPSILON)
    scores = raw * c_scale_col * (q_scale_row * INVERSE)
    ids = jnp.where(sub < BANK, sub + pa * BANK, -1)
    counts = jnp.where((sub >= BANK) & (sub < BANK + SHARE), 1.0, 0.0)
    for k in range(NEG):
        counts = counts + jnp.where(neg[k:k + 1, :] == ids, 1.0, 0.0)
    exps_t = jnp.exp(scores) * counts
    total_part[...] = jnp.broadcast_to(jnp.sum(exps_t, axis=0, keepdims=True), (8, ROWS))
    totals[pl.ds(pa, 1)] = total_part[...][None]

    pl.semaphore_wait(barrier, len(partners) + jnp.where(z == HUB, NZ - 1, 0))

    @pl.when(z == HUB)
    def _():
        for step in range(1, NZ):
            pl.semaphore_signal(all_here, inc=1, device_id=at_z(step), device_id_type=MESH)


    for place in range(NY - 1):
        pltpu.make_async_remote_copy(
            src_ref=total_part, dst_ref=totals.at[pa],
            send_sem=t_send_sem, recv_sem=t_recv_sem,
            device_id=(pb, place + jnp.where(place >= pa, 1, 0)), device_id_type=MESH).start()

    weight = jnp.transpose(exps_t * c_scale_col).astype(BF16)

    def part_half(half):
        for block in range(HALF // 256):
            cols = pl.ds(half * HALF + block * 256, 256)
            part[:, cols] = jnp.dot(weight, rows[ROWS:, cols], preferred_element_type=F32)

    def y_rows(step):
        return pl.ds(pl.multiple_of(((pa + step) % NY) * SHARE, SHARE), SHARE)

    def y_distance(m):
        return 4 - (m + 1) // 2

    def y_half(s, m):
        return s if m % 2 == 0 else 1 - s

    def y_copy(s, m):
        sign = 1 if s == 0 else -1
        return pltpu.make_async_remote_copy(
            src_ref=part.at[y_rows((sign * y_distance(m)) % NY), pl.ds(y_half(s, m) * HALF, HALF)],
            dst_ref=y_recv.at[s, m],
            send_sem=y_send_sem, recv_sem=y_recv_sem.at[s, m],
            device_id=at_y(sign % NY), device_id_type=MESH)

    for s in range(2):
        part_half(s)
        y_copy(s, 0).start()
    for s in range(2):
        y_copy(s, 1).start()

    def y_step(m):
        for s in range(2):
            y_copy(s, m).wait_recv()
            sign = 1 if s == 0 else -1
            dest = y_rows((sign * (y_distance(m) - 1)) % NY)
            cols = pl.ds(y_half(s, m) * HALF, HALF)
            part[dest, cols] = part[dest, cols] + y_recv[s, m]
            y_copy(s, m + 2).start()

    place = sub % BATCH_ROWS
    place_core, place_x, place_z = place // HALF_ROWS, (place % HALF_ROWS) // CHUNK, place % CHUNK
    bank_row = place_x * (NZ * NC) + ((sub // BATCH_ROWS) * GROUP + place_z) * NC + place_core
    order = jnp.where(sub < BANK, bank_row, sub)
    move = jnp.where(lane == order, 1.0, 0.0).astype(BF16)
    high = exps_t.astype(BF16)
    rest = exps_t - high.astype(F32)
    middle = rest.astype(BF16)
    low = (rest - middle.astype(F32)).astype(BF16)
    ordered = (jnp.dot(move, high, preferred_element_type=F32)
               + jnp.dot(move, middle, preferred_element_type=F32)
               + jnp.dot(move, low, preferred_element_type=F32))

    arrive(totals.at[1:NY], t_recv_sem)
    total_row = jnp.sum(totals[...], axis=0)[0:1, :]
    weight_t = (ordered * (q_scale_row * INVERSE / total_row)).astype(BF16)

    def core_rows(which):
        return pl.ds(pl.multiple_of(which * (HALF_ROWS * SUB), HALF_ROWS * SUB), HALF_ROWS * SUB)

    def c_copy(piece):
        return pltpu.make_async_remote_copy(
            src_ref=bank.at[piece, core_rows(1 - core)], dst_ref=c_recv.at[piece],
            send_sem=c_send_sem, recv_sem=c_recv_sem.at[piece // 2],
            device_id=other_core, device_id_type=MESH)

    for half in range(2):
        for block in range(HALF // 256):
            cols = pl.ds(half * HALF + block * 256, 256)
            product = jnp.dot(weight_t, rows[0:ROWS, cols], preferred_element_type=F32)
            passage_up[:, cols] = product[BANK:BANK + SHARE, :]
            for r in range(BANK // 8):
                batch, r8 = r // (BATCH_ROWS // 8), r % (BATCH_ROWS // 8)
                for c in range(2):
                    bank[2 * batch + half, pl.ds(r8 * 8 * SUB + block * 2 + c, 8, stride=SUB), :] = (
                        product[r * 8:r * 8 + 8, c * 128:c * 128 + 128])
        c_copy(half).start()
    for piece in range(2, NT):
        c_copy(piece).start()

    def x_rows(step):
        start = core * (HALF_ROWS * SUB) + ((x + step) % NX) * (CHUNK * SUB)
        return pl.ds(pl.multiple_of(start, CHUNK * SUB), CHUNK * SUB)

    def x_send(stage, piece, s):
        sign = 1 if s == 0 else -1
        recv_sem = x1_recv_sem if stage == 1 else x2_recv_sem
        pltpu.make_async_remote_copy(
            src_ref=bank.at[piece, x_rows(2 if stage == 1 else sign % NX)],
            dst_ref=x_recv1.at[piece] if stage == 1 else x_recv2.at[piece, s],
            send_sem=x_send_sem.at[stage - 1], recv_sem=recv_sem.at[piece // 2],
            device_id=at_x(sign % NX), device_id_type=MESH).start()

    def c_step(batch):
        arrive(c_recv.at[2 * batch:2 * batch + 2], c_recv_sem.at[batch])
        own = core_rows(core)
        for piece in (2 * batch, 2 * batch + 1):
            bank[piece, own, :] = bank[piece, own, :] + c_recv[piece]

    def x_first(batch, stage):
        for s in range(2):
            x_send(stage, 2 * batch + (s if stage == 1 else 1 - s), s)

    def x1_step(batch):
        arrive(x_recv1.at[2 * batch:2 * batch + 2], x1_recv_sem.at[batch])
        for s in range(2):
            piece = 2 * batch + s
            dest = x_rows((1 if s == 0 else -1) % NX)
            bank[piece, dest, :] = bank[piece, dest, :] + x_recv1[piece]
            x_send(2, piece, s)

    def x2_step(batch):
        arrive(x_recv2.at[2 * batch:2 * batch + 2], x2_recv_sem.at[batch])
        for s in range(2):
            piece = 2 * batch + s
            total = bank[piece, x_rows(0), :] + x_recv2[piece, 0] + x_recv2[piece, 1]
            z_send[batch * GROUP:(batch + 1) * GROUP, s * SUB:(s + 1) * SUB, :] = total.reshape(CHUNK, SUB, 128)
        for target in range(batch * GROUP, (batch + 1) * GROUP):
            @pl.when(z != target)
            def _():
                pltpu.make_async_remote_copy(
                    src_ref=z_send.at[target], dst_ref=z_recv.at[z],
                    send_sem=z_send_sem, recv_sem=z_recv_sem,
                    device_id=((x * NZ + target) * NC + core, pa), device_id_type=MESH).start()

    def norm_back(wide, scale, upstream):
        inner = jnp.sum(wide * upstream, axis=1, keepdims=True)
        return scale * upstream - (scale * scale * scale * inner) * wide

    own_lane, own_sub = iota((SHARE, ROWS), 1), iota((SHARE, ROWS), 0)
    own_query = own_lane == own_sub + pa * SHARE
    q_scale_own = pick(own_query, q_scale_row, 1)
    total_own = pick(own_query, total_row, 1)
    p_scale_own = pick(own_lane == own_sub + BANK, c_scale_row, 1)

    c_step(0)
    x_first(0, 1)
    x_first(0, 2)
    y_step(0)
    c_step(1)
    c_step(2)
    c_step(3)
    x1_step(0)
    x_first(1, 1)
    x_first(1, 2)
    x_first(2, 1)
    y_step(1)

    @pl.when(z != HUB)
    def _():
        pl.semaphore_wait(all_here, 1)

    x2_step(0)
    y_step(2)
    x1_step(1)
    x_first(2, 2)
    x_first(3, 1)
    x2_step(1)
    x1_step(2)
    x_first(3, 2)
    y_step(3)
    x1_step(3)
    x2_step(2)
    x2_step(3)
    z_recv[pl.ds(z, 1)] = z_send[pl.ds(z, 1)]

    own_q_rows = pl.ds(pl.multiple_of(pa * SHARE, SHARE), SHARE)
    own_q = rows[own_q_rows, :].astype(F32)
    own_p = rows[ROWS + BANK:ROWS + BANK + SHARE, :].astype(F32)
    passage_v = passage_up[...] - own_q * (q_scale_own * INVERSE)
    out_p[...] = norm_back(own_p, p_scale_own, passage_v)
    store_p = pltpu.make_async_copy(out_p, pg_hbm, store_sem.at[0])
    store_p.start()
    own_score = pick(own_query, scores[BANK:BANK + SHARE, :], 1)
    loss = pick(own_lane == own_sub, jnp.log(total_own) - own_score, 0)
    out_loss[...] = loss[:, :SHARE]
    store_loss = pltpu.make_async_copy(out_loss, loss_hbm, store_sem.at[1])
    store_loss.start()


    y_step(4)

    one_hot = jnp.where(iota((SHARE, ROWS), 1) == pb, 1.0, 0.0).astype(BF16)
    for block in range(D // 256):
        row = jnp.dot(one_hot, rows[ROWS:, block * 256:block * 256 + 256], preferred_element_type=F32)
        for c in range(2):
            own_row[block * 2 + c:block * 2 + c + 1, :] = row[0:1, c * 128:c * 128 + 128]


    inverse_own = INVERSE / total_own
    own = y_rows(0)
    inner = jnp.zeros((SHARE, 1), F32)
    for m in (5, 6):
        for s in range(2):
            y_copy(s, m).wait_recv()
    for half in range(2):
        cols = slice(half * HALF, (half + 1) * HALF)
        arrived = y_recv[0, 6 if half == 0 else 5] + y_recv[1, 5 if half == 0 else 6]
        value = (part[own, cols] + arrived) * inverse_own
        value = value - own_p[:, cols] * (p_scale_own * INVERSE)
        out_q[:, cols] = value
        inner = inner + jnp.sum(value * own_q[:, cols], axis=1, keepdims=True)
    out_q[...] = q_scale_own * out_q[...] - (q_scale_own * q_scale_own * q_scale_own * inner) * own_q
    store_q = pltpu.make_async_copy(out_q, qg_hbm, store_sem.at[3])
    store_q.start()

    def whole(values):
        return jnp.sum(jnp.sum(values, axis=0, keepdims=True), axis=1, keepdims=True)

    wide = own_row[...]
    scale = lax.rsqrt(whole(wide * wide) + EPSILON)
    arrive(totals.at[1:NY], t_send_sem)
    arrive(y_recv, y_send_sem)
    arrive(c_recv, c_send_sem)
    arrive(x_recv2, x_send_sem.at[1])
    arrive(z_send.at[1:NZ], z_send_sem)
    arrive(x_recv1, x_send_sem.at[0])
    for store in (store_p, store_loss, store_q):
        store.wait()

    arrive(z_recv.at[1:NZ], z_recv_sem)
    bank_v = jnp.sum(z_recv[...], axis=0)
    out_b[...] = scale * bank_v - (scale * scale * scale * whole(wide * bank_v)) * wide
    store_b = pltpu.make_async_copy(out_b, bg_hbm, store_sem.at[2])
    store_b.start()
    store_b.wait()


def hand_over(*refs):
    copies = [pltpu.make_async_copy(refs[i], refs[4 + i], refs[8].at[i]) for i in range(4)]
    for copy in copies:
        copy.start()
    for copy in copies:
        copy.wait()


def on_device(queries, positives, negative_pool, negatives):
    anywhere = pl.BlockSpec(memory_space=pl.ANY)
    dma = pltpu.SemaphoreType.DMA
    query_grad, positive_grad, pool_grad, losses = pl.pallas_call(
        kernel,
        out_shape=(
            jax.ShapeDtypeStruct((SHARE, D), F32),
            jax.ShapeDtypeStruct((SHARE, D), F32),
            jax.ShapeDtypeStruct((D // 128, 128), F32),
            jax.ShapeDtypeStruct((1, SHARE), F32),
        ),
        in_specs=[anywhere] * 4,
        out_specs=(anywhere,) * 4,
        scratch_shapes=[
            pltpu.VMEM((2 * ROWS, D), BF16),
            pltpu.VMEM((NEG, ROWS), jnp.int32),
            pltpu.VMEM((ROWS, D), F32),
            pltpu.VMEM((D // 128, 128), F32),
            pltpu.VMEM((SHARE, D), F32),
            pltpu.VMEM((SHARE, D), F32),
            pltpu.VMEM((SHARE, D), F32),
            pltpu.VMEM((D // 128, 128), F32),
            pltpu.VMEM((1, SHARE), F32),
            pltpu.VMEM((NY, 8, ROWS), F32),
            pltpu.VMEM((8, ROWS), F32),
            pltpu.VMEM((2, 7, SHARE, HALF), F32),
            pltpu.VMEM((NT, BATCH_ROWS * SUB, 128), F32),
            pltpu.VMEM((NT, HALF_ROWS * SUB, 128), F32),
            pltpu.VMEM((NT, CHUNK * SUB, 128), F32),
            pltpu.VMEM((NT, 2, CHUNK * SUB, 128), F32),
            pltpu.VMEM((NZ, D // 128, 128), F32),
            pltpu.VMEM((NZ, D // 128, 128), F32),
            dma((2,)), dma((4,)), dma, dma, dma, dma((2, 7)),
            dma, dma((NB,)), dma((2,)), dma((NB,)), dma((NB,)),
            dma, dma, pltpu.SemaphoreType.REGULAR,
        ],
        compiler_params=pltpu.CompilerParams(
            collective_id=0, has_side_effects=True, vmem_limit_bytes=40 * 1024 * 1024),
    )(*[pltpu.with_memory_space_constraint(t, pltpu.HBM) for t in (queries, positives, negative_pool, negatives.T)])
    query_grad, positive_grad, pool_grad, losses = pl.pallas_call(
        hand_over,
        out_shape=(
            jax.ShapeDtypeStruct((SHARE, D), F32),
            jax.ShapeDtypeStruct((SHARE, D), F32),
            jax.ShapeDtypeStruct((D // 128, 128), F32),
            jax.ShapeDtypeStruct((1, SHARE), F32),
        ),
        in_specs=[anywhere] * 4,
        out_specs=(anywhere,) * 4,
        scratch_shapes=[dma((4,))],
        compiler_params=pltpu.CompilerParams(vmem_limit_bytes=4 * 1024 * 1024),
    )(query_grad, positive_grad, pool_grad, losses)
    return query_grad, positive_grad, pool_grad.reshape(1, 1, D), losses.reshape(SHARE)


def solution(mesh):
    placed = (P("pb", None), P(("pb", "pa"), None), P("pa", None), P("pb", None))
    return jax.shard_map(
        on_device,
        mesh=mesh,
        in_specs=placed,
        out_specs=(
            P(("pb", "pa"), None),
            P(("pb", "pa"), None),
            P("pa", "pb", None),
            P(("pb", "pa")),
        ),
        check_vma=False,
    )
```
